512 devices in a mesh: tok: 64 (over x, y, z_lo), voc: 8 (over z_hi, core).
Axes of the slice: x: 4, y: 8, z: 8 (z_hi: 4, z_lo: 2; z = z_hi * 2 + z_lo), core: 2. Of those that a mesh axis runs over, the one named last changes fastest.
Arguments:
- teacher_hidden: bfloat16 [65536, 4608], P(('tok', 'voc')), may hold values from -512 to 512
- student_hidden: bfloat16 [65536, 2304], P(('tok', 'voc')), may hold values from -512 to 512
- teacher_head: bfloat16 [2048, 4608], P('voc'), may hold values from -1 to 1
- student_head: bfloat16 [2304, 2048], P('tok', 'voc'), may hold values from -1 to 1
- targets: int32 [65536], P(('tok', 'voc')), may hold values from 0 to 2047
- row_mask: int32 [65536], P(('tok', 'voc')), may hold values 0 or 1
Outputs:
- row_loss: float32 [65536], P(('tok', 'voc'))
- head_grad: float32 [2304, 2048], P('tok', 'voc')
The draws below stay inside these ranges and needn't reach their ends.
All inputs are finite; a program needn't handle non-finite values. No bound on the sum of `row_mask` on one device may be relied on, other than what follows from the above.
Results may differ from the reference program's by a relative error of at most 0.0022.
Values may be sent and summed in bfloat16 or wider, within the bound.
A program may use at most 64 MiB of HBM per device.

```python
import math
import jax
import jax.numpy as jnp
import numpy as np
from jax import lax

DT = 4608
DS = 2304
VOCAB = 2048
TOKENS = 65536


def teacher_matrix(key):
    return jnp.clip(jax.random.normal(jax.random.fold_in(key, 101), (VOCAB, DT), jnp.float32), -6.0, 6.0) * DT ** (-0.5)


def student_matrix(key):
    return jnp.clip(jax.random.normal(jax.random.fold_in(key, 102), (VOCAB, DS), jnp.float32), -6.0, 6.0) * DS ** (-0.5)


def hidden_rows(key, width):
    first = jax.random.fold_in(key, 0)
    return 3.0 * jnp.clip(jax.random.normal(first, (TOKENS, width), jnp.float32), -6.0, 6.0)


def draw_teacher_head(key, part):
    matrix = teacher_matrix(key)
    return matrix.astype(jnp.bfloat16)


def draw_student_head(key, part):
    matrix = student_matrix(key)
    return matrix.T.astype(jnp.bfloat16)


def draw_teacher_hidden(key, part):
    key = jax.random.fold_in(key, 3)
    return hidden_rows(key, DT).astype(jnp.bfloat16)


def draw_student_hidden(key, part):
    key = jax.random.fold_in(key, 4)
    return hidden_rows(key, DS).astype(jnp.bfloat16)


def set_ends(result, rng, low, top_value):
    index_at = [jax.random.randint(jax.random.fold_in(rng, axis), (), 0, length) for axis, length in enumerate(result.shape)]
    longest = result.shape.index(max(result.shape))
    next_to = index_at[:longest] + [(index_at[longest] + 1) % result.shape[longest]] + index_at[longest + 1:]
    return result.at[tuple(index_at)].set(low).at[tuple(next_to)].set(top_value)


def rank_bounds(count, lean):
    loads = [(1 << 20) // math.isqrt(standing ** lean) + 1 for standing in range(1, count + 1)]
    deviation = 1 + sum(loads) // (1 << 30)
    return np.cumsum(np.array([max(1, weight // deviation) for weight in loads]))


def ranked(stream_key, dims, number_of, slope):
    listing = rank_bounds(number_of, slope)
    ticket = jax.random.randint(jax.random.fold_in(stream_key, 1), dims, 0, int(listing[number_of - 1]))
    rank = jnp.searchsorted(jnp.asarray(listing, jnp.int32), ticket, side="right")
    return jax.random.permutation(jax.random.fold_in(stream_key, 2), number_of)[rank].astype(jnp.int32)


def setup_inputs(seed: int = 0) -> dict:
    key_list = jax.random.split(jax.random.key(seed), 7)
    return {
        "teacher_hidden": draw_teacher_hidden(jax.random.fold_in(key_list[6], 71), 0),
        "student_hidden": draw_student_hidden(jax.random.fold_in(key_list[6], 71), 0),
        "teacher_head": draw_teacher_head(jax.random.fold_in(key_list[6], 71), 0),
        "student_head": draw_student_head(jax.random.fold_in(key_list[6], 71), 0),
        "targets": set_ends(ranked(key_list[4], (TOKENS,), VOCAB, 2), jax.random.fold_in(key_list[4], 3), 0, VOCAB - 1).astype(jnp.int32),
        "row_mask": set_ends((jax.random.randint(key_list[5], (TOKENS,), 0, 4) < 3).astype(jnp.int32), jax.random.fold_in(key_list[5], 1), 0, 1),
    }


def reference(teacher_hidden, student_hidden, teacher_head, student_head, targets, row_mask):
    block = math.gcd(TOKENS, 2048)
    count = TOKENS // block
    teach = teacher_hidden.reshape(count, block, DT)
    stud = student_hidden.reshape(count, block, DS)
    labels = targets.reshape(count, block)
    masks = row_mask.reshape(count, block)
    column = jnp.arange(VOCAB, dtype=jnp.int32)

    def step(total, item):
        rows_t, rows_s, label, mask = item
        tl = jnp.dot(rows_t, teacher_head.T, preferred_element_type=jnp.float32)
        sl = jnp.dot(rows_s, student_head, preferred_element_type=jnp.float32)
        top_t = jnp.max(tl, axis=1)
        top_s = jnp.max(sl, axis=1)
        exp_t = jnp.exp(tl - top_t[:, None])
        exp_s = jnp.exp(sl - top_s[:, None])
        sum_t = jnp.sum(exp_t, axis=1)
        sum_s = jnp.sum(exp_s, axis=1)
        cross_sum = jnp.sum(exp_t * (tl - sl), axis=1)
        lse_t = top_t + jnp.log(sum_t)
        lse_s = top_s + jnp.log(sum_s)
        onehot = (label[:, None] == column[None, :]).astype(jnp.float32)
        target_logit = jnp.sum(onehot * sl, axis=1)
        weight = mask.astype(jnp.float32)
        loss = weight * (cross_sum / sum_t - lse_t + lse_s + 0.5 * (lse_s - target_logit))
        prob_t = exp_t / sum_t[:, None]
        prob_s = exp_s / sum_s[:, None]
        grad = (weight[:, None] * ((prob_s - prob_t) + 0.5 * (prob_s - onehot))).astype(jnp.bfloat16)
        total = total + jnp.dot(rows_s.T, grad, preferred_element_type=jnp.float32)
        return total, loss

    start = jnp.zeros((DS, VOCAB), jnp.float32)
    total, losses = lax.scan(step, start, (teach, stud, labels, masks))
    return losses.reshape(TOKENS), total
```

```python
import jax
import jax.numpy as jnp
from jax import lax
from jax.experimental import pallas as pl
from jax.experimental.pallas import tpu as pltpu
from jax.sharding import PartitionSpec as P

NX, NY, NZ = 4, 8, 8
ROWS = 128
HALF = ROWS // 2
SLAB = 256
PIECE = 36
PAD = 48
WIN = 40
MESH = pl.DeviceIdType.MESH
F32 = jnp.float32
NT = (((1,), (1,)), ((), ()))


def remote(src, dst, send, recv, device):
    return pltpu.make_async_remote_copy(
        src_ref=src, dst_ref=dst, send_sem=send, recv_sem=recv, device_id=device, device_id_type=MESH
    )


def kernel(
    th, sh, tw, sw, lab_in, loss_ref, out_ref,
    rt, rs, tslab, spad, swt, et, es, lg, g, yb, zb, ow, ox, labs, stats, losses,
    loc_sem, lab_s, lab_r, tr_s, tr_r, zt_s, zt_r, zs_s, zs_r, y_s, y_r,
    x_s, x_r, f_s, f_r, b_s, b_r, st_s, st_r, ys_s, ys_r, zr_s, zr_r, o_s, o_r,
):
    tok, voc = lax.axis_index("tok"), lax.axis_index("voc")
    x, y, zl = lax.div(tok, 16), lax.rem(lax.div(tok, 2), NY), lax.rem(tok, 2)
    zh, c = lax.div(voc, 2), lax.rem(voc, 2)
    z = zh * 2 + zl
    me = x * 2 + c

    def dev(dx, dy, dz, dc):
        return ((dx * NY + dy) * 2 + lax.rem(dz, 2), lax.div(dz, 2) * 2 + dc)

    def group_dev(i):
        return dev(lax.div(i, 2), y, z, lax.rem(i, 2))

    xr, xl, xo = lax.rem(x + 1, NX), lax.rem(x + 3, NX), lax.rem(x + 2, NX)
    right, left, sib = dev(xr, y, z, c), dev(xl, y, z, c), dev(x, y, z, 1 - c)
    up, down = dev(x, lax.rem(y + 1, NY), z, c), dev(x, lax.rem(y + NY - 1, NY), z, c)
    partner = dev(zh, y, x * 2 + zl, c)
    away = x != zh

    barrier = pltpu.get_barrier_semaphore()

    def greet(k, _):
        pl.semaphore_signal(barrier, inc=1, device_id=group_dev(lax.rem(me + k, 8)), device_id_type=MESH)
        pl.semaphore_signal(barrier, inc=1, device_id=dev(x, y, lax.rem(z + k, NZ), c), device_id_type=MESH)
        return 0

    lax.fori_loop(1, 8, greet, 0)
    pl.semaphore_signal(barrier, inc=1, device_id=up, device_id_type=MESH)
    pl.semaphore_signal(barrier, inc=1, device_id=down, device_id_type=MESH)

    @pl.when(away)
    def _():
        pl.semaphore_signal(barrier, inc=1, device_id=partner, device_id_type=MESH)

    @pl.when(away)
    def _():
        pl.semaphore_wait(barrier, 17)

    @pl.when(jnp.logical_not(away))
    def _():
        pl.semaphore_wait(barrier, 16)

    t_row = pl.multiple_of(y * 32 + zl * 16, 16)

    def t_piece(ref, col):
        return ref.at[pl.ds(t_row, 16), pl.ds(pl.multiple_of(col * 1152, 128), 1152)]

    def turn(dst_col):
        src_t, dst_t = t_piece(tw, x), t_piece(tslab, dst_col)
        dst_s = spad.at[y, dst_col, zl]
        return src_t, dst_t, dst_s

    def turn_copies():
        src_t, dst_t, dst_s = turn(x)
        return (
            remote(src_t, dst_t, tr_s.at[0], tr_r.at[0], partner),
            remote(sw, dst_s, tr_s.at[1], tr_r.at[1], partner),
        )

    def turn_local():
        src_t, dst_t, dst_s = turn(x)
        return (
            pltpu.make_async_copy(src_t, dst_t, loc_sem.at[2]),
            pltpu.make_async_copy(sw, dst_s, loc_sem.at[3]),
        )

    @pl.when(away)
    def _():
        for copy in turn_copies():
            copy.start()

    @pl.when(jnp.logical_not(away))
    def _():
        for copy in turn_local():
            copy.start()

    def half(ref, block, h):
        return ref.at[block, pl.ds(h * HALF, HALF)]

    pairs = ((sh, rs), (th, rt))

    def send_own(d, h, a):
        src, dst = pairs[a]
        return remote(
            src.at[pl.ds(h * HALF, HALF)], half(dst, me, h), x_s.at[d, h, a], x_r.at[d, h, a], (right, left)[d]
        )

    def came_own(d, h, a):
        block = (xl, xr)[d] * 2 + c
        piece = half(pairs[a][1], block, h)
        return remote(piece, piece, x_s.at[d, h, a], x_r.at[d, h, a], (right, left)[d])

    def pass_on(d, a):
        block = (xl, xr)[d] * 2 + c
        piece = half(pairs[a][1], block, d)
        return remote(piece, piece, f_s.at[d, a], f_r.at[d, a], (right, left)[d])

    def came_on(d, a):
        piece = half(pairs[a][1], xo * 2 + c, d)
        return remote(piece, piece, f_s.at[d, a], f_r.at[d, a], (right, left)[d])

    def to_sib(n, block, h, a):
        piece = half(pairs[a][1], block * 2 + c, h)
        return remote(piece, piece, b_s.at[n, h, a], b_r.at[n, h, a], sib)

    def from_sib(n, block, h, a):
        piece = half(pairs[a][1], block * 2 + 1 - c, h)
        return remote(piece, piece, b_s.at[n, h, a], b_r.at[n, h, a], sib)

    def own_to_sib(h, a):
        src, dst = pairs[a]
        return remote(src.at[pl.ds(h * HALF, HALF)], half(dst, me, h), b_s.at[0, h, a], b_r.at[0, h, a], sib)

    for first in (0, 1):
        for a in (0, 1):
            send_own(0, first, a).start()
            send_own(1, 1 - first, a).start()
    own_copies = [pltpu.make_async_copy(pairs[a][0], pairs[a][1].at[me], loc_sem.at[a]) for a in (0, 1)]
    for copy in own_copies:
        copy.start()
    for h in (0, 1):
        for a in (0, 1):
            own_to_sib(h, a).start()

    def send_labels(k, _):
        to = lax.rem(me + k, 8)
        remote(lab_in, labs.at[me], lab_s.at[k], lab_r.at[me], group_dev(to)).start()
        return 0

    lax.fori_loop(1, 8, send_labels, 0)
    labs[me] = lab_in[...]

    @pl.when(away)
    def _():
        for copy in turn_copies():
            copy.wait_send()
        src_t, dst_t, dst_s = turn(zh)
        remote(dst_t, dst_t, tr_s.at[0], tr_r.at[0], partner).wait_recv()
        remote(dst_s, dst_s, tr_s.at[1], tr_r.at[1], partner).wait_recv()

    @pl.when(jnp.logical_not(away))
    def _():
        for copy in turn_local():
            copy.wait()

    def z_piece(dz):
        col, low = lax.div(dz, 2), lax.rem(dz, 2)
        rows = pl.ds(pl.multiple_of(y * 32 + low * 16, 16), 16)
        return (
            tslab.at[rows, pl.ds(pl.multiple_of(col * 1152, 128), 1152)],
            spad.at[y, col, low],
        )

    def z_copies(k, slot, index):
        to = lax.rem(z + k, NZ)
        t, s = z_piece(slot)
        d = dev(x, y, to, c)
        return remote(t, t, zt_s.at[k], zt_r.at[index], d), remote(s, s, zs_s.at[k], zs_r.at[index], d)

    def z_start(k, _):
        for copy in z_copies(k, z, z):
            copy.start()
        return 0

    def z_wait(k, _):
        other = lax.rem(z + k, NZ)
        for copy in z_copies(k, other, other):
            copy.wait_recv()
        return 0

    lax.fori_loop(1, NZ, z_start, 0)
    lax.fori_loop(1, NZ, z_wait, 0)

    def y_copies(d, step, chunk):
        to = (up, down)[d]
        sems = y_s.at[d, step, 0], y_r.at[d, step, 0], y_s.at[d, step, 1], y_r.at[d, step, 1]
        if step < 3:
            t = tslab.at[pl.ds(pl.multiple_of(chunk * 32, 32), 32)]
            s = spad.at[chunk]
        else:
            t = tslab.at[pl.ds(pl.multiple_of(chunk * 32 + 16 * d, 16), 16)]
            s = spad.at[chunk, pl.ds(2 * d, 2)]
        return remote(t, t, sems[0], sems[1], to), remote(s, s, sems[2], sems[3], to)

    def y_start(step):
        for d in (0, 1):
            chunk = lax.rem(y + (NY - step, step)[d], NY)
            for copy in y_copies(d, step, chunk):
                copy.start()

    def y_wait(step):
        for d in (0, 1):
            chunk = lax.rem(y + (NY - step - 1, step + 1)[d], NY)
            for copy in y_copies(d, step, chunk):
                copy.wait_recv()

    y_start(0)
    y_wait(0)
    y_start(1)
    for a in (0, 1):
        for d in (0, 1):
            came_own(d, d, a).wait_recv()
            pass_on(d, a).start()
            to_sib(1 + d, (xl, xr)[d], d, a).start()
    y_wait(1)
    y_start(2)
    for a in (0, 1):
        for d in (0, 1):
            came_own(d, 1 - d, a).wait_recv()
            to_sib(1 + d, (xl, xr)[d], 1 - d, a).start()
    y_wait(2)
    y_start(3)
    y_wait(3)

    r_out = lax.broadcasted_iota(jnp.int32, (4 * PAD, 4 * PIECE), 1)
    r_in = lax.broadcasted_iota(jnp.int32, (4 * PAD, 4 * PIECE), 0)
    quarter = lax.div(r_out, PIECE)
    pick = (r_in == quarter * PAD + (r_out - quarter * PIECE)).astype(jnp.bfloat16)

    for col in range(NX):
        parts = []
        for pair in range(NY // 2):
            padded = spad[2 * pair : 2 * pair + 2, col].reshape(4 * PAD, SLAB)
            parts.append(lax.dot_general(pick, padded, (((0,), (0,)), ((), ())), preferred_element_type=F32))
        swt[576 * col : 576 * (col + 1), :] = jnp.concatenate(parts, axis=0).astype(jnp.bfloat16)

    def wait_labels(k, _):
        other = lax.rem(me + k, 8)
        remote(labs.at[other], labs.at[other], lab_s.at[k], lab_r.at[other], sib).wait_recv()
        return 0

    lax.fori_loop(1, 8, wait_labels, 0)
    for copy in own_copies:
        copy.wait()
    for h in (0, 1):
        for a in (0, 1):
            from_sib(0, x, h, a).wait_recv()

    entry = lax.broadcasted_iota(jnp.int32, (SLAB, 2 * ROWS), 0) + me * SLAB

    def label_row(block, i):
        return jnp.concatenate([labs[2 * block, i : i + 1, :], labs[2 * block + 1, i : i + 1, :]], axis=1)

    def logits(block):
        rows_t = rt[pl.ds(2 * block, 2)].reshape(2 * ROWS, rt.shape[2])
        lt = lax.dot_general(tslab[...], rows_t, NT, preferred_element_type=F32)
        rows_s = rs[pl.ds(2 * block, 2)].reshape(2 * ROWS, rs.shape[2])
        ls = lax.dot_general(swt[...], rows_s, (((0,), (1,)), ((), ())), preferred_element_type=F32)
        top_t = jnp.max(lt, axis=0, keepdims=True)
        top_s = jnp.max(ls, axis=0, keepdims=True)
        exp_t, exp_s = jnp.exp(lt - top_t), jnp.exp(ls - top_s)
        hit = entry == label_row(block, 0)
        et[block] = exp_t
        es[block] = exp_s
        stats[me, block] = jnp.concatenate(
            [
                top_t,
                top_s,
                jnp.sum(exp_t, axis=0, keepdims=True),
                jnp.sum(exp_t * (lt - ls), axis=0, keepdims=True),
                jnp.sum(exp_s, axis=0, keepdims=True),
                jnp.sum(jnp.where(hit, ls, 0.0), axis=0, keepdims=True),
                jnp.zeros((2, 2 * ROWS), F32),
            ],
            axis=0,
        )

    logits(x)
    for d in (0, 1):
        for h in (0, 1):
            for a in (0, 1):
                from_sib(1 + d, (xl, xr)[d], h, a).wait_recv()
        logits((xl, xr)[d])
    for a in (0, 1):
        for d in (0, 1):
            came_on(d, a).wait_recv()
            to_sib(3, xo, d, a).start()
    for d in (0, 1):
        for a in (0, 1):
            from_sib(3, xo, d, a).wait_recv()
    logits(xo)

    def send_stats(k, _):
        remote(stats.at[me], stats.at[me], st_s.at[k], st_r.at[me], group_dev(lax.rem(me + k, 8))).start()
        return 0

    def wait_stats(k, _):
        other = lax.rem(me + k, 8)
        remote(stats.at[other], stats.at[other], st_s.at[k], st_r.at[other], sib).wait_recv()
        return 0

    lax.fori_loop(1, 8, send_stats, 0)
    lax.fori_loop(1, 8, wait_stats, 0)

    for block in range(NX):
        tops_t, tops_s = stats[:, block, 0, :], stats[:, block, 1, :]
        top_t = jnp.max(tops_t, axis=0, keepdims=True)
        top_s = jnp.max(tops_s, axis=0, keepdims=True)
        scale_t, scale_s = jnp.exp(tops_t - top_t), jnp.exp(tops_s - top_s)
        sum_t = jnp.sum(stats[:, block, 2, :] * scale_t, axis=0, keepdims=True)
        cross = jnp.sum(stats[:, block, 3, :] * scale_t, axis=0, keepdims=True)
        sum_s = jnp.sum(stats[:, block, 4, :] * scale_s, axis=0, keepdims=True)
        target = jnp.sum(stats[:, block, 5, :], axis=0, keepdims=True)
        lse_t, lse_s = top_t + jnp.log(sum_t), top_s + jnp.log(sum_s)
        weight = label_row(block, 1).astype(F32)
        loss = weight * (cross / sum_t - lse_t + lse_s + 0.5 * (lse_s - target))
        losses[2 * block] = loss[:, :ROWS]
        losses[2 * block + 1] = loss[:, ROWS:]
        prob_t = et[block] * (jnp.exp(stats[me, block, 0:1, :] - top_t) / sum_t)
        prob_s = es[block] * (jnp.exp(stats[me, block, 1:2, :] - top_s) / sum_s)
        onehot = (entry == label_row(block, 0)).astype(F32)
        grad = weight * ((prob_s - prob_t) + 0.5 * (prob_s - onehot))
        lg[:, 2 * ROWS * block : 2 * ROWS * (block + 1)] = grad.astype(jnp.bfloat16)
    loss_ref[...] = losses[me]

    def grad_tile(j, _):
        cols = pl.ds(pl.multiple_of(j * 256, 256), 256)
        rows_s = rs[:, :, cols].reshape(8 * ROWS, 256)
        g[cols, :] = lax.dot_general(rows_s.T, lg[...], NT, preferred_element_type=F32)
        return 0

    lax.fori_loop(0, g.shape[0] // 256, grad_tile, 0)

    def g_chunk(stream, chunk):
        return pl.ds(pl.multiple_of(stream * 576 + chunk * 72, 8), 72)

    def ring_copy(stream, step, src):
        return remote(
            src, yb.at[step, stream], ys_s.at[step, stream], ys_r.at[step, stream], (up, down)[stream // 2]
        )

    for stream in range(4):
        first = lax.rem(y + (NY - 1, 1)[stream // 2], NY)
        ring_copy(stream, 0, g.at[g_chunk(stream, first)]).start()

    def ring_add(stream, step):
        ring_copy(stream, step, yb.at[step, stream]).wait_recv()
        gap = step + 2
        chunk = lax.rem(y + (2 * NY - gap, gap)[stream // 2], NY)
        yb[step, stream] += g[g_chunk(stream, chunk), :]

    def ring_step(step, _):
        for stream in (0, 2, 1, 3):
            ring_add(stream, step)
            ring_copy(stream, step + 1, yb.at[step, stream]).start()
        return 0

    lax.fori_loop(0, NY - 2, ring_step, 0)
    for stream in (0, 2, 1, 3):
        ring_add(stream, NY - 2)

    def window(dz):
        return yb.at[NY - 2, lax.div(dz, 2), pl.ds(pl.multiple_of(lax.rem(dz, 2) * 32, 8), WIN)]

    def zr_start(k, _):
        to = lax.rem(z + k, NZ)
        remote(window(to), zb.at[z], zr_s.at[k], zr_r.at[z], dev(x, y, to, c)).start()
        return 0

    def zr_wait(k, _):
        other = lax.rem(z + k, NZ)
        remote(zb.at[other], zb.at[other], zr_s.at[k], zr_r.at[other], sib).wait_recv()
        return 0

    lax.fori_loop(1, NZ, zr_start, 0)
    zb[z] = window(z)[...]
    lax.fori_loop(1, NZ, zr_wait, 0)
    ow[...] = jnp.sum(zb[...], axis=0)

    @pl.when(away)
    def _():
        copy = remote(ow, ox, o_s, o_r, partner)
        copy.start()
        copy.wait()
        out_ref[...] = ox[...]

    @pl.when(jnp.logical_not(away))
    def _():
        out_ref[...] = ow[...]

    for d in (0, 1):
        for a in (0, 1):
            for h in (0, 1):
                send_own(d, h, a).wait_send()
            pass_on(d, a).wait_send()
    for a in (0, 1):
        for h in (0, 1):
            own_to_sib(h, a).wait_send()
            for n, block in ((1, xl), (2, xr), (3, xo)):
                to_sib(n, block, h, a).wait_send()
    for step in range(4):
        for d in (0, 1):
            for copy in y_copies(d, step, lax.rem(y + (NY - step, step)[d], NY)):
                copy.wait_send()

    def wait_sent(k, _):
        remote(lab_in, labs.at[me], lab_s.at[k], lab_r.at[me], sib).wait_send()
        for copy in z_copies(k, z, z):
            copy.wait_send()
        remote(stats.at[me], stats.at[me], st_s.at[k], st_r.at[me], sib).wait_send()
        remote(window(lax.rem(z + k, NZ)), zb.at[z], zr_s.at[k], zr_r.at[z], sib).wait_send()
        return 0

    lax.fori_loop(1, 8, wait_sent, 0)

    def wait_ring(step, _):
        for stream in range(4):
            ring_copy(stream, step, yb.at[step, stream]).wait_send()
        return 0

    lax.fori_loop(0, NY - 1, wait_ring, 0)


def per_device(teacher_hidden, student_hidden, teacher_head, student_head, targets, row_mask):
    dt, ds = teacher_hidden.shape[1], student_hidden.shape[1]
    bf16 = jnp.bfloat16
    labels = jnp.concatenate([targets[None], row_mask[None], jnp.zeros((6, ROWS), jnp.int32)], axis=0)
    padded = jnp.concatenate([student_head, jnp.zeros((PAD - PIECE, SLAB), bf16)], axis=0)
    dma = pltpu.SemaphoreType.DMA
    anywhere, vmem = pl.BlockSpec(memory_space=pl.ANY), pl.BlockSpec(memory_space=pltpu.VMEM)
    loss, window = pl.pallas_call(
        kernel,
        out_shape=(jax.ShapeDtypeStruct((1, ROWS), F32), jax.ShapeDtypeStruct((WIN, SLAB), F32)),
        in_specs=[anywhere, anywhere, anywhere, vmem, vmem],
        out_specs=(vmem, vmem),
        scratch_shapes=[
            pltpu.VMEM((8, ROWS, dt), bf16),
            pltpu.VMEM((8, ROWS, ds), bf16),
            pltpu.VMEM((SLAB, dt), bf16),
            pltpu.VMEM((NY, NX, 2, PAD, SLAB), bf16),
            pltpu.VMEM((ds, SLAB), bf16),
            pltpu.VMEM((NX, SLAB, 2 * ROWS), F32),
            pltpu.VMEM((NX, SLAB, 2 * ROWS), F32),
            pltpu.VMEM((SLAB, 8 * ROWS), bf16),
            pltpu.VMEM((ds, SLAB), F32),
            pltpu.VMEM((NY - 1, 4, 72, SLAB), F32),
            pltpu.VMEM((NZ, WIN, SLAB), F32),
            pltpu.VMEM((WIN, SLAB), F32),
            pltpu.VMEM((WIN, SLAB), F32),
            pltpu.VMEM((8, 8, ROWS), jnp.int32),
            pltpu.VMEM((8, NX, 8, 2 * ROWS), F32),
            pltpu.VMEM((8, 1, ROWS), F32),
            dma((4,)),
            dma((8,)), dma((8,)),
            dma((2,)), dma((2,)),
            dma((8,)), dma((8,)), dma((8,)), dma((8,)),
            dma((2, 4, 2)), dma((2, 4, 2)),
            dma((2, 2, 2)), dma((2, 2, 2)),
            dma((2, 2)), dma((2, 2)),
            dma((4, 2, 2)), dma((4, 2, 2)),
            dma((8,)), dma((8,)),
            dma((7, 4)), dma((7, 4)),
            dma((8,)), dma((8,)),
            dma, dma,
        ],
        compiler_params=pltpu.CompilerParams(
            collective_id=0, has_side_effects=True, vmem_limit_bytes=56 * 1024 * 1024
        ),
        cost_estimate=pl.CostEstimate(flops=4_900_000_000, bytes_accessed=6_000_000, transcendentals=1_000_000),
    )(teacher_hidden, student_hidden, teacher_head, padded, labels)
    low = lax.rem(lax.axis_index("tok"), 2)
    return loss.reshape(ROWS), lax.dynamic_slice_in_dim(window, low * (WIN - PIECE), PIECE, 0)


def solution(mesh):
    in_specs = (
        P(("tok", "voc"), None),
        P(("tok", "voc"), None),
        P("voc", None),
        P("tok", "voc"),
        P(("tok", "voc")),
        P(("tok", "voc")),
    )
    out_specs = (P(("tok", "voc")), P("tok", "voc"))
    return jax.shard_map(
        per_device, mesh=mesh, in_specs=in_specs, out_specs=out_specs, check_vma=False
    )
```

```python
import jax
import jax.numpy as jnp
from jax import lax
from jax.experimental import pallas as pl
from jax.experimental.pallas import tpu as pltpu
from jax.sharding import PartitionSpec as P

NX, NY, NZ = 4, 8, 8
ROWS = 128
HALF = ROWS // 2
SLAB = 256
PIECE = 36
PAD = 48
WIN = 40
MESH = pl.DeviceIdType.MESH
F32 = jnp.float32
NT = (((1,), (1,)), ((), ()))


def remote(src, dst, send, recv, device):
    return pltpu.make_async_remote_copy(
        src_ref=src, dst_ref=dst, send_sem=send, recv_sem=recv, device_id=device, device_id_type=MESH
    )


def kernel(
    th, sh, tw, sw, target_in, mask_in, loss_ref, out_ref,
    rt, rs, piece_ref, tslab, spad, swt, et, es, lg, g, yb, zb, y2, z2, ow, ox, labs, stats, losses,
    loc_sem, lab_s, lab_r, tr_s, tr_r, zt_s, zt_r, zs_s, zs_r, y_s, y_r,
    x_s, x_r, f_s, f_r, b_s, b_r, st_s, st_r, ys_s, ys_r, zq_s, zq_r, yr_s, yr_r, zr_s, zr_r, o_s, o_r,
):
    tok, voc = lax.axis_index("tok"), lax.axis_index("voc")
    x, y, zl = lax.div(tok, 16), lax.rem(lax.div(tok, 2), NY), lax.rem(tok, 2)
    zh, c = lax.div(voc, 2), lax.rem(voc, 2)
    z = zh * 2 + zl
    me = x * 2 + c

    def dev(dx, dy, dz, dc):
        return ((dx * NY + dy) * 2 + lax.rem(dz, 2), lax.div(dz, 2) * 2 + dc)

    def group_dev(i):
        return dev(lax.div(i, 2), y, z, lax.rem(i, 2))

    xr, xl, xo = lax.rem(x + 1, NX), lax.rem(x + 3, NX), lax.rem(x + 2, NX)
    right, left, sib = dev(xr, y, z, c), dev(xl, y, z, c), dev(x, y, z, 1 - c)
    up, down = dev(x, lax.rem(y + 1, NY), z, c), dev(x, lax.rem(y + NY - 1, NY), z, c)
    z_up, z_down = dev(x, y, lax.rem(z + 1, NZ), c), dev(x, y, lax.rem(z + NZ - 1, NZ), c)
    partner = dev(zh, y, x * 2 + zl, c)
    away = x != zh

    barrier = pltpu.get_barrier_semaphore()

    def greet(k, _):
        pl.semaphore_signal(barrier, inc=1, device_id=group_dev(lax.rem(me + k, 8)), device_id_type=MESH)
        pl.semaphore_signal(barrier, inc=1, device_id=dev(x, y, lax.rem(z + k, NZ), c), device_id_type=MESH)
        pl.semaphore_signal(barrier, inc=1, device_id=dev(x, lax.rem(y + k, NY), z, c), device_id_type=MESH)
        return 0

    lax.fori_loop(1, 8, greet, 0)

    @pl.when(away)
    def _():
        pl.semaphore_signal(barrier, inc=1, device_id=partner, device_id_type=MESH)

    own_copies = [pltpu.make_async_copy(ref, dst.at[me], loc_sem.at[a]) for a, (ref, dst) in enumerate(((sh, rs), (th, rt)))]
    for copy in own_copies:
        copy.start()
    piece_ref[...] = jnp.concatenate([sw[...], jnp.zeros((PAD - PIECE, SLAB), sw.dtype)], axis=0)
    labs[me] = jnp.concatenate([target_in[...], mask_in[...], jnp.zeros((6, ROWS), jnp.int32)], axis=0)

    @pl.when(away)
    def _():
        pl.semaphore_wait(barrier, 22)

    @pl.when(jnp.logical_not(away))
    def _():
        pl.semaphore_wait(barrier, 21)

    t_row = pl.multiple_of(y * 32 + zl * 16, 16)

    def t_piece(ref, col):
        return ref.at[pl.ds(t_row, 16), pl.ds(pl.multiple_of(col * 1152, 128), 1152)]

    def turn(dst_col):
        src_t, dst_t = t_piece(tw, x), t_piece(tslab, dst_col)
        dst_s = spad.at[y, dst_col, zl]
        return src_t, dst_t, dst_s

    def turn_copies():
        src_t, dst_t, dst_s = turn(x)
        return (
            remote(src_t, dst_t, tr_s.at[0], tr_r.at[0], partner),
            remote(piece_ref, dst_s, tr_s.at[1], tr_r.at[1], partner),
        )

    def turn_local():
        src_t, dst_t, dst_s = turn(x)
        return (
            pltpu.make_async_copy(src_t, dst_t, loc_sem.at[2]),
            pltpu.make_async_copy(piece_ref, dst_s, loc_sem.at[3]),
        )

    @pl.when(away)
    def _():
        for copy in turn_copies():
            copy.start()

    @pl.when(jnp.logical_not(away))
    def _():
        for copy in turn_local():
            copy.start()

    def half(ref, block, h):
        return ref.at[block, pl.ds(h * HALF, HALF)]

    pairs = ((sh, rs), (th, rt))

    def send_own(d, h, a):
        src, dst = pairs[a]
        return remote(
            src.at[pl.ds(h * HALF, HALF)], half(dst, me, h), x_s.at[d, h, a], x_r.at[d, h, a], (right, left)[d]
        )

    def came_own(d, h, a):
        block = (xl, xr)[d] * 2 + c
        piece = half(pairs[a][1], block, h)
        return remote(piece, piece, x_s.at[d, h, a], x_r.at[d, h, a], (right, left)[d])

    def pass_on(d, a):
        block = (xl, xr)[d] * 2 + c
        piece = half(pairs[a][1], block, d)
        return remote(piece, piece, f_s.at[d, a], f_r.at[d, a], (right, left)[d])

    def came_on(d, a):
        piece = half(pairs[a][1], xo * 2 + c, d)
        return remote(piece, piece, f_s.at[d, a], f_r.at[d, a], (right, left)[d])

    def to_sib(n, block, h, a):
        piece = half(pairs[a][1], block * 2 + c, h)
        return remote(piece, piece, b_s.at[n, h, a], b_r.at[n, h, a], sib)

    def from_sib(n, block, h, a):
        piece = half(pairs[a][1], block * 2 + 1 - c, h)
        return remote(piece, piece, b_s.at[n, h, a], b_r.at[n, h, a], sib)

    def own_to_sib(h, a):
        src, dst = pairs[a]
        return remote(src.at[pl.ds(h * HALF, HALF)], half(dst, me, h), b_s.at[0, h, a], b_r.at[0, h, a], sib)

    for first in (0, 1):
        for a in (0, 1):
            send_own(0, first, a).start()
            send_own(1, 1 - first, a).start()
    for h in (0, 1):
        for a in (0, 1):
            own_to_sib(h, a).start()

    def send_labels(k, _):
        to = lax.rem(me + k, 8)
        remote(labs.at[me], labs.at[me], lab_s.at[k], lab_r.at[me], group_dev(to)).start()
        return 0

    lax.fori_loop(1, 8, send_labels, 0)

    @pl.when(away)
    def _():
        for copy in turn_copies():
            copy.wait_send()
        src_t, dst_t, dst_s = turn(zh)
        remote(dst_t, dst_t, tr_s.at[0], tr_r.at[0], partner).wait_recv()
        remote(dst_s, dst_s, tr_s.at[1], tr_r.at[1], partner).wait_recv()

    @pl.when(jnp.logical_not(away))
    def _():
        for copy in turn_local():
            copy.wait()

    def z_piece(dz):
        col, low = lax.div(dz, 2), lax.rem(dz, 2)
        rows = pl.ds(pl.multiple_of(y * 32 + low * 16, 16), 16)
        return (
            tslab.at[rows, pl.ds(pl.multiple_of(col * 1152, 128), 1152)],
            spad.at[y, col, low],
        )

    def z_copies(k, slot, index):
        to = lax.rem(z + k, NZ)
        t, s = z_piece(slot)
        d = dev(x, y, to, c)
        return remote(t, t, zt_s.at[k], zt_r.at[index], d), remote(s, s, zs_s.at[k], zs_r.at[index], d)

    def z_start(k, _):
        for copy in z_copies(k, z, z):
            copy.start()
        return 0

    def z_wait(k, _):
        other = lax.rem(z + k, NZ)
        for copy in z_copies(k, other, other):
            copy.wait_recv()
        return 0

    lax.fori_loop(1, NZ, z_start, 0)
    lax.fori_loop(1, NZ, z_wait, 0)

    def y_copies(d, step, chunk):
        to = (up, down)[d]
        sems = y_s.at[d, step, 0], y_r.at[d, step, 0], y_s.at[d, step, 1], y_r.at[d, step, 1]
        if step < 3:
            t = tslab.at[pl.ds(pl.multiple_of(chunk * 32, 32), 32)]
            s = spad.at[chunk]
        else:
            t = tslab.at[pl.ds(pl.multiple_of(chunk * 32 + 16 * d, 16), 16)]
            s = spad.at[chunk, pl.ds(2 * d, 2)]
        return remote(t, t, sems[0], sems[1], to), remote(s, s, sems[2], sems[3], to)

    def y_start(step):
        for d in (0, 1):
            chunk = lax.rem(y + (NY - step, step)[d], NY)
            for copy in y_copies(d, step, chunk):
                copy.start()

    def y_wait(step):
        for d in (0, 1):
            chunk = lax.rem(y + (NY - step - 1, step + 1)[d], NY)
            for copy in y_copies(d, step, chunk):
                copy.wait_recv()

    y_start(0)
    y_wait(0)
    y_start(1)
    for a in (0, 1):
        for d in (0, 1):
            came_own(d, d, a).wait_recv()
            pass_on(d, a).start()
            to_sib(1 + d, (xl, xr)[d], d, a).start()
    y_wait(1)
    y_start(2)
    for a in (0, 1):
        for d in (0, 1):
            came_own(d, 1 - d, a).wait_recv()
            to_sib(1 + d, (xl, xr)[d], 1 - d, a).start()
    y_wait(2)
    y_start(3)
    y_wait(3)

    r_out = lax.broadcasted_iota(jnp.int32, (4 * PAD, 4 * PIECE), 1)
    r_in = lax.broadcasted_iota(jnp.int32, (4 * PAD, 4 * PIECE), 0)
    quarter = lax.div(r_out, PIECE)
    pick = (r_in == quarter * PAD + (r_out - quarter * PIECE)).astype(jnp.bfloat16)

    for col in range(NX):
        parts = []
        for pair in range(NY // 2):
            padded = spad[2 * pair : 2 * pair + 2, col].reshape(4 * PAD, SLAB)
            parts.append(lax.dot_general(pick, padded, (((0,), (0,)), ((), ())), preferred_element_type=F32))
        swt[576 * col : 576 * (col + 1), :] = jnp.concatenate(parts, axis=0).astype(jnp.bfloat16)

    def wait_labels(k, _):
        other = lax.rem(me + k, 8)
        remote(labs.at[other], labs.at[other], lab_s.at[k], lab_r.at[other], sib).wait_recv()
        return 0

    lax.fori_loop(1, 8, wait_labels, 0)
    for copy in own_copies:
        copy.wait()
    for h in (0, 1):
        for a in (0, 1):
            from_sib(0, x, h, a).wait_recv()

    entry = lax.broadcasted_iota(jnp.int32, (SLAB, 2 * ROWS), 0) + me * SLAB

    def label_row(block, i):
        return jnp.concatenate([labs[2 * block, i : i + 1, :], labs[2 * block + 1, i : i + 1, :]], axis=1)

    def logits(block):
        rows_t = rt[pl.ds(2 * block, 2)].reshape(2 * ROWS, rt.shape[2])
        lt = lax.dot_general(tslab[...], rows_t, NT, preferred_element_type=F32)
        rows_s = rs[pl.ds(2 * block, 2)].reshape(2 * ROWS, rs.shape[2])
        ls = lax.dot_general(swt[...], rows_s, (((0,), (1,)), ((), ())), preferred_element_type=F32)
        top_t = jnp.max(lt, axis=0, keepdims=True)
        top_s = jnp.max(ls, axis=0, keepdims=True)
        exp_t, exp_s = jnp.exp(lt - top_t), jnp.exp(ls - top_s)
        hit = entry == label_row(block, 0)
        et[block] = exp_t
        es[block] = exp_s
        stats[me, block] = jnp.concatenate(
            [
                top_t,
                top_s,
                jnp.sum(exp_t, axis=0, keepdims=True),
                jnp.sum(exp_t * (lt - ls), axis=0, keepdims=True),
                jnp.sum(exp_s, axis=0, keepdims=True),
                jnp.sum(jnp.where(hit, ls, 0.0), axis=0, keepdims=True),
                jnp.zeros((2, 2 * ROWS), F32),
            ],
            axis=0,
        )

    logits(x)
    for d in (0, 1):
        for h in (0, 1):
            for a in (0, 1):
                from_sib(1 + d, (xl, xr)[d], h, a).wait_recv()
        logits((xl, xr)[d])
    for a in (0, 1):
        for d in (0, 1):
            came_on(d, a).wait_recv()
            to_sib(3, xo, d, a).start()
    for d in (0, 1):
        for a in (0, 1):
            from_sib(3, xo, d, a).wait_recv()
    logits(xo)

    def send_stats(k, _):
        remote(stats.at[me], stats.at[me], st_s.at[k], st_r.at[me], group_dev(lax.rem(me + k, 8))).start()
        return 0

    def wait_stats(k, _):
        other = lax.rem(me + k, 8)
        remote(stats.at[other], stats.at[other], st_s.at[k], st_r.at[other], sib).wait_recv()
        return 0

    lax.fori_loop(1, 8, send_stats, 0)
    lax.fori_loop(1, 8, wait_stats, 0)

    for block in range(NX):
        tops_t, tops_s = stats[:, block, 0, :], stats[:, block, 1, :]
        top_t = jnp.max(tops_t, axis=0, keepdims=True)
        top_s = jnp.max(tops_s, axis=0, keepdims=True)
        scale_t, scale_s = jnp.exp(tops_t - top_t), jnp.exp(tops_s - top_s)
        sum_t = jnp.sum(stats[:, block, 2, :] * scale_t, axis=0, keepdims=True)
        cross = jnp.sum(stats[:, block, 3, :] * scale_t, axis=0, keepdims=True)
        sum_s = jnp.sum(stats[:, block, 4, :] * scale_s, axis=0, keepdims=True)
        target = jnp.sum(stats[:, block, 5, :], axis=0, keepdims=True)
        lse_t, lse_s = top_t + jnp.log(sum_t), top_s + jnp.log(sum_s)
        weight = label_row(block, 1).astype(F32)
        loss = weight * (cross / sum_t - lse_t + lse_s + 0.5 * (lse_s - target))
        losses[2 * block] = loss[:, :ROWS]
        losses[2 * block + 1] = loss[:, ROWS:]
        prob_t = et[block] * (jnp.exp(stats[me, block, 0:1, :] - top_t) / sum_t)
        prob_s = es[block] * (jnp.exp(stats[me, block, 1:2, :] - top_s) / sum_s)
        onehot = (entry == label_row(block, 0)).astype(F32)
        grad = weight * ((prob_s - prob_t) + 0.5 * (prob_s - onehot))
        lg[:, 2 * ROWS * block : 2 * ROWS * (block + 1)] = grad.astype(jnp.bfloat16)
    loss_ref[...] = losses[me]

    half_cols = g.shape[0] // 2 * g.shape[1] * g.shape[2]
    for j in range(2):
        rows_s = rs[:, :, half_cols * j : half_cols * (j + 1)].reshape(8 * ROWS, half_cols)
        tile = lax.dot_general(rows_s.T, lg[...], NT, preferred_element_type=F32)
        g[2 * j : 2 * j + 2] = tile.reshape((2,) + g.shape[1:])

    def y_ring(stream, step, src):
        return remote(
            src, yb.at[step, stream], ys_s.at[step, stream], ys_r.at[step, stream], (up, down)[stream // 2]
        )

    def z_ring(stream, step, src):
        return remote(
            src, zb.at[step, stream], zq_s.at[step, stream], zq_r.at[step, stream], (z_up, z_down)[stream // 2]
        )

    def at_step(base, stream, step):
        gap = step + 1
        return lax.rem(base + (16 - gap, gap)[stream // 2], 8)

    def y_view(stream, chunk):
        return g.at[stream, chunk, :, pl.ds(0, 128)]

    def z_view(stream, chunk):
        low = pl.multiple_of(lax.rem(chunk, 2) * 32, 8)
        return g.at[lax.div(chunk, 2), pl.ds(2 * stream, 2), pl.ds(low, WIN), pl.ds(128, 128)]

    for stream in (0, 2, 1, 3):
        y_ring(stream, 0, y_view(stream, at_step(y, stream, 0))).start()
        z_ring(stream, 0, z_view(stream, at_step(z, stream, 0))).start()

    def ring_add(stream, step):
        y_ring(stream, step, yb.at[step, stream]).wait_recv()
        yb[step, stream] += y_view(stream, at_step(y, stream, step + 1))[...]

    def z_add(stream, step):
        z_ring(stream, step, zb.at[step, stream]).wait_recv()
        zb[step, stream] += z_view(stream, at_step(z, stream, step + 1))[...]

    def ring_step(step, _):
        for stream in (0, 2, 1, 3):
            ring_add(stream, step)
            y_ring(stream, step + 1, yb.at[step, stream]).start()
            z_add(stream, step)
            z_ring(stream, step + 1, zb.at[step, stream]).start()
        return 0

    lax.fori_loop(0, NY - 2, ring_step, 0)
    for stream in (0, 2, 1, 3):
        ring_add(stream, NY - 2)
        z_add(stream, NY - 2)

    def y_done(dz):
        return yb.at[NY - 2, lax.div(dz, 2), pl.ds(pl.multiple_of(lax.rem(dz, 2) * 32, 8), WIN)]

    def z_done(dy):
        return zb.at[NZ - 2, lax.div(dy, 2), lax.rem(dy, 2)]

    def last_copies(k):
        to_z, to_y = lax.rem(z + k, NZ), lax.rem(y + k, NY)
        return (
            remote(y_done(to_z), y2.at[z], zr_s.at[k], zr_r.at[z], dev(x, y, to_z, c)),
            remote(z_done(to_y), z2.at[y], yr_s.at[k], yr_r.at[y], dev(x, to_y, z, c)),
        )

    def last_start(k, _):
        for copy in last_copies(k):
            copy.start()
        return 0

    def last_wait(k, _):
        from_z, from_y = lax.rem(z + k, NZ), lax.rem(y + k, NY)
        remote(y2.at[from_z], y2.at[from_z], zr_s.at[k], zr_r.at[from_z], sib).wait_recv()
        remote(z2.at[from_y], z2.at[from_y], yr_s.at[k], yr_r.at[from_y], sib).wait_recv()
        return 0

    lax.fori_loop(1, 8, last_start, 0)
    y2[z] = y_done(z)[...]
    z2[y] = z_done(y)[...]
    lax.fori_loop(1, 8, last_wait, 0)
    ow[...] = jnp.concatenate([jnp.sum(y2[...], axis=0), jnp.sum(z2[...], axis=0)], axis=1)

    @pl.when(away)
    def _():
        copy = remote(ow, ox, o_s, o_r, partner)
        copy.start()
        copy.wait()

    @pl.when(jnp.logical_not(away))
    def _():
        ox[...] = ow[...]

    out_ref[...] = jnp.where(zl == 0, ox[:PIECE], ox[WIN - PIECE :])

    for d in (0, 1):
        for a in (0, 1):
            for h in (0, 1):
                send_own(d, h, a).wait_send()
            pass_on(d, a).wait_send()
    for a in (0, 1):
        for h in (0, 1):
            own_to_sib(h, a).wait_send()
            for n, block in ((1, xl), (2, xr), (3, xo)):
                to_sib(n, block, h, a).wait_send()
    for step in range(4):
        for d in (0, 1):
            for copy in y_copies(d, step, lax.rem(y + (NY - step, step)[d], NY)):
                copy.wait_send()

    def wait_sent(k, _):
        remote(labs.at[me], labs.at[me], lab_s.at[k], lab_r.at[me], sib).wait_send()
        for copy in z_copies(k, z, z):
            copy.wait_send()
        remote(stats.at[me], stats.at[me], st_s.at[k], st_r.at[me], sib).wait_send()
        for copy in last_copies(k):
            copy.wait_send()
        return 0

    lax.fori_loop(1, 8, wait_sent, 0)

    def wait_ring(step, _):
        for stream in range(4):
            y_ring(stream, step, yb.at[step, stream]).wait_send()
            z_ring(stream, step, zb.at[step, stream]).wait_send()
        return 0

    lax.fori_loop(0, NY - 1, wait_ring, 0)


def per_device(teacher_hidden, student_hidden, teacher_head, student_head, targets, row_mask):
    dt, ds = teacher_hidden.shape[1], student_hidden.shape[1]
    bf16 = jnp.bfloat16
    dma = pltpu.SemaphoreType.DMA
    anywhere, vmem = pl.BlockSpec(memory_space=pl.ANY), pl.BlockSpec(memory_space=pltpu.VMEM)
    loss, out = pl.pallas_call(
        kernel,
        out_shape=(jax.ShapeDtypeStruct((1, ROWS), F32), jax.ShapeDtypeStruct((PIECE, SLAB), F32)),
        in_specs=[anywhere, anywhere, anywhere, vmem, vmem, vmem],
        out_specs=(vmem, vmem),
        scratch_shapes=[
            pltpu.VMEM((8, ROWS, dt), bf16),
            pltpu.VMEM((8, ROWS, ds), bf16),
            pltpu.VMEM((PAD, SLAB), bf16),
            pltpu.VMEM((SLAB, dt), bf16),
            pltpu.VMEM((NY, NX, 2, PAD, SLAB), bf16),
            pltpu.VMEM((ds, SLAB), bf16),
            pltpu.VMEM((NX, SLAB, 2 * ROWS), F32),
            pltpu.VMEM((NX, SLAB, 2 * ROWS), F32),
            pltpu.VMEM((SLAB, 8 * ROWS), bf16),
            pltpu.VMEM((NX, NY, 2 * PIECE, SLAB), F32),
            pltpu.VMEM((NY - 1, 4, 2 * PIECE, 128), F32),
            pltpu.VMEM((NZ - 1, 4, 2, WIN, 128), F32),
            pltpu.VMEM((NZ, WIN, 128), F32),
            pltpu.VMEM((NY, WIN, 128), F32),
            pltpu.VMEM((WIN, SLAB), F32),
            pltpu.VMEM((WIN, SLAB), F32),
            pltpu.VMEM((8, 8, ROWS), jnp.int32),
            pltpu.VMEM((8, NX, 8, 2 * ROWS), F32),
            pltpu.VMEM((8, 1, ROWS), F32),
            dma((4,)),
            dma((8,)), dma((8,)),
            dma((2,)), dma((2,)),
            dma((8,)), dma((8,)), dma((8,)), dma((8,)),
            dma((2, 4, 2)), dma((2, 4, 2)),
            dma((2, 2, 2)), dma((2, 2, 2)),
            dma((2, 2)), dma((2, 2)),
            dma((4, 2, 2)), dma((4, 2, 2)),
            dma((8,)), dma((8,)),
            dma((7, 4)), dma((7, 4)), dma((7, 4)), dma((7, 4)),
            dma((8,)), dma((8,)), dma((8,)), dma((8,)),
            dma, dma,
        ],
        compiler_params=pltpu.CompilerParams(
            collective_id=0, has_side_effects=True, vmem_limit_bytes=56 * 1024 * 1024
        ),
        cost_estimate=pl.CostEstimate(flops=4_900_000_000, bytes_accessed=6_000_000, transcendentals=1_000_000),
    )(teacher_hidden, student_hidden, teacher_head, student_head, targets.reshape(1, ROWS), row_mask.reshape(1, ROWS))
    return loss.reshape(ROWS), out


def solution(mesh):
    in_specs = (
        P(("tok", "voc"), None),
        P(("tok", "voc"), None),
        P("voc", None),
        P("tok", "voc"),
        P(("tok", "voc")),
        P(("tok", "voc")),
    )
    out_specs = (P(("tok", "voc")), P("tok", "voc"))
    return jax.shard_map(
        per_device, mesh=mesh, in_specs=in_specs, out_specs=out_specs, check_vma=False
    )
```

```python
import jax
import jax.numpy as jnp
from jax import lax
from jax.experimental import pallas as pl
from jax.experimental.pallas import tpu as pltpu
from jax.sharding import PartitionSpec as P

NX, NY, NZ = 4, 8, 8
ROWS = 128
HALF = ROWS // 2
SLAB = 256
PIECE = 36
PAD = 48
WIN = 40
TALL, WIN16 = 80, 48
MESH = pl.DeviceIdType.MESH
F32 = jnp.float32
NT = (((1,), (1,)), ((), ()))


def remote(src, dst, send, recv, device):
    return pltpu.make_async_remote_copy(
        src_ref=src, dst_ref=dst, send_sem=send, recv_sem=recv, device_id=device, device_id_type=MESH
    )


def kernel(
    th, sh, tw, sw, target_in, mask_in, loss_ref, out_ref,
    rt, rs, piece_ref, tslab, spad, swt, swr, rst, et, es, lg, g, gb, yq, zq, ya, za, y2, z2, ow, ox, labs, stats, late, losses,
    loc_sem, lab_s, lab_r, tr_s, tr_r, zt_s, zt_r, zs_s, zs_r, h_s, h_r,
    x_s, x_r, f_s, f_r, b_s, b_r, st_s, st_r, sl_s, sl_r, ys_s, ys_r, zq_s, zq_r, yr_s, yr_r, zr_s, zr_r, o_s, o_r,
):
    tok, voc = lax.axis_index("tok"), lax.axis_index("voc")
    x, y, zl = lax.div(tok, 16), lax.rem(lax.div(tok, 2), NY), lax.rem(tok, 2)
    zh, c = lax.div(voc, 2), lax.rem(voc, 2)
    z = zh * 2 + zl
    me = x * 2 + c

    def dev(dx, dy, dz, dc):
        return ((dx * NY + dy) * 2 + lax.rem(dz, 2), lax.div(dz, 2) * 2 + dc)

    def group_dev(i):
        return dev(lax.div(i, 2), y, z, lax.rem(i, 2))

    xr, xl, xo = lax.rem(x + 1, NX), lax.rem(x + 3, NX), lax.rem(x + 2, NX)
    right, left, sib = dev(xr, y, z, c), dev(xl, y, z, c), dev(x, y, z, 1 - c)
    up, down = dev(x, lax.rem(y + 1, NY), z, c), dev(x, lax.rem(y + NY - 1, NY), z, c)
    z_up, z_down = dev(x, y, lax.rem(z + 1, NZ), c), dev(x, y, lax.rem(z + NZ - 1, NZ), c)
    partner = dev(zh, y, x * 2 + zl, c)
    away = x != zh

    barrier = pltpu.get_barrier_semaphore()

    def greet(k, _):
        pl.semaphore_signal(barrier, inc=1, device_id=group_dev(lax.rem(me + k, 8)), device_id_type=MESH)
        pl.semaphore_signal(barrier, inc=1, device_id=dev(x, y, lax.rem(z + k, NZ), c), device_id_type=MESH)
        pl.semaphore_signal(barrier, inc=1, device_id=dev(x, lax.rem(y + k, NY), z, c), device_id_type=MESH)
        return 0

    lax.fori_loop(1, 8, greet, 0)

    @pl.when(away)
    def _():
        pl.semaphore_signal(barrier, inc=1, device_id=partner, device_id_type=MESH)

    own_copies = [pltpu.make_async_copy(ref, dst.at[me], loc_sem.at[a]) for a, (ref, dst) in enumerate(((sh, rs), (th, rt)))]
    for copy in own_copies:
        copy.start()
    piece_ref[...] = jnp.concatenate([sw[...], jnp.zeros((PAD - PIECE, SLAB), sw.dtype)], axis=0)
    stats[me] = jnp.zeros(stats.shape[1:], F32)
    labs[me] = jnp.concatenate([target_in[...], mask_in[...], jnp.zeros((6, ROWS), jnp.int32)], axis=0)

    @pl.when(away)
    def _():
        pl.semaphore_wait(barrier, 22)

    @pl.when(jnp.logical_not(away))
    def _():
        pl.semaphore_wait(barrier, 21)

    t_row = pl.multiple_of(y * 32 + zl * 16, 16)

    def t_piece(ref, col):
        return ref.at[pl.ds(t_row, 16), pl.ds(pl.multiple_of(col * 1152, 128), 1152)]

    def turn(dst_col):
        src_t, dst_t = t_piece(tw, x), t_piece(tslab, dst_col)
        dst_s = spad.at[dst_col * 2 + zl, y]
        return src_t, dst_t, dst_s

    def turn_copies():
        src_t, dst_t, dst_s = turn(x)
        return (
            remote(src_t, dst_t, tr_s.at[0], tr_r.at[0], partner),
            remote(piece_ref, dst_s, tr_s.at[1], tr_r.at[1], partner),
        )

    def turn_local():
        src_t, dst_t, dst_s = turn(x)
        return (
            pltpu.make_async_copy(src_t, dst_t, loc_sem.at[2]),
            pltpu.make_async_copy(piece_ref, dst_s, loc_sem.at[3]),
        )

    @pl.when(away)
    def _():
        for copy in turn_copies():
            copy.start()

    @pl.when(jnp.logical_not(away))
    def _():
        for copy in turn_local():
            copy.start()

    def half(ref, block, h):
        return ref.at[block, pl.ds(h * HALF, HALF)]

    pairs = ((sh, rs), (th, rt))

    def send_own(d, h, a):
        src, dst = pairs[a]
        return remote(
            src.at[pl.ds(h * HALF, HALF)], half(dst, me, h), x_s.at[d, h, a], x_r.at[d, h, a], (right, left)[d]
        )

    def came_own(d, h, a):
        block = (xl, xr)[d] * 2 + c
        piece = half(pairs[a][1], block, h)
        return remote(piece, piece, x_s.at[d, h, a], x_r.at[d, h, a], (right, left)[d])

    def pass_on(d, a):
        block = (xl, xr)[d] * 2 + c
        piece = half(pairs[a][1], block, d)
        return remote(piece, piece, f_s.at[d, a], f_r.at[d, a], (right, left)[d])

    def came_on(d, a):
        piece = half(pairs[a][1], xo * 2 + c, d)
        return remote(piece, piece, f_s.at[d, a], f_r.at[d, a], (right, left)[d])

    def to_sib(n, block, h, a):
        piece = half(pairs[a][1], block * 2 + c, h)
        return remote(piece, piece, b_s.at[n, h, a], b_r.at[n, h, a], sib)

    def from_sib(n, block, h, a):
        piece = half(pairs[a][1], block * 2 + 1 - c, h)
        return remote(piece, piece, b_s.at[n, h, a], b_r.at[n, h, a], sib)

    def own_to_sib(h, a):
        src, dst = pairs[a]
        return remote(src.at[pl.ds(h * HALF, HALF)], half(dst, me, h), b_s.at[0, h, a], b_r.at[0, h, a], sib)

    for first in (0, 1):
        for a in (0, 1):
            send_own(0, first, a).start()
            send_own(1, 1 - first, a).start()
    for h in (0, 1):
        for a in (0, 1):
            own_to_sib(h, a).start()

    def send_labels(k, _):
        to = lax.rem(me + k, 8)
        remote(labs.at[me], labs.at[me], lab_s.at[k], lab_r.at[me], group_dev(to)).start()
        return 0

    lax.fori_loop(1, 8, send_labels, 0)

    @pl.when(away)
    def _():
        for copy in turn_copies():
            copy.wait_send()
        src_t, dst_t, dst_s = turn(zh)
        remote(dst_t, dst_t, tr_s.at[0], tr_r.at[0], partner).wait_recv()
        remote(dst_s, dst_s, tr_s.at[1], tr_r.at[1], partner).wait_recv()

    @pl.when(jnp.logical_not(away))
    def _():
        for copy in turn_local():
            copy.wait()

    def z_piece(dz):
        rows = pl.ds(pl.multiple_of(y * 32 + lax.rem(dz, 2) * 16, 16), 16)
        return tslab.at[rows, pl.ds(pl.multiple_of(lax.div(dz, 2) * 1152, 128), 1152)]

    def z_copies(k, back):
        dz, dy = lax.rem(z + k, NZ), lax.rem(y + k, NY)
        sz, sy = (dz, dy) if back else (z, y)
        t, s = z_piece(sz), spad.at[z, sy]
        return (
            remote(t, t, zt_s.at[k], zt_r.at[sz], dev(x, y, dz, c)),
            remote(s, s, zs_s.at[k], zs_r.at[sy], dev(x, dy, z, c)),
        )

    def z_start(k, _):
        for copy in z_copies(k, False):
            copy.start()
        return 0

    def z_wait(k, _):
        for copy in z_copies(k, True):
            copy.wait_recv()
        return 0

    lax.fori_loop(1, NZ, z_start, 0)
    lax.fori_loop(1, NZ, z_wait, 0)

    def ring_copy(a, d, step, h, back):
        gap = step + 1 if back else step
        move = (8 - gap, gap)[d]
        if a == 0:
            chunk = lax.rem(y + move, NY)
            piece = tslab.at[pl.ds(pl.multiple_of(chunk * 32 + 16 * h, 16), 16)]
        else:
            piece = spad.at[lax.rem(z + move, NZ), pl.ds(4 * h, 4)]
        to = ((up, down), (z_up, z_down))[a][d]
        return remote(piece, piece, h_s.at[a, d, step, h], h_r.at[a, d, step, h], to)

    def ring_step(step):
        for h in (0, 1):
            for d in (0, 1):
                for a in (0, 1):
                    if 0 < step < 4 or (step == 4 and h == d):
                        ring_copy(a, d, step - 1, h, True).wait_recv()
                    if step < 3 or (step == 3 and h == d):
                        ring_copy(a, d, step, h, False).start()

    ring_step(0)
    ring_step(1)
    for a in (0, 1):
        for d in (0, 1):
            came_own(d, d, a).wait_recv()
            pass_on(d, a).start()
            to_sib(1 + d, (xl, xr)[d], d, a).start()
    ring_step(2)
    ring_step(3)
    for a in (0, 1):
        for d in (0, 1):
            came_own(d, 1 - d, a).wait_recv()
            to_sib(1 + d, (xl, xr)[d], 1 - d, a).start()
    ring_step(4)

    r_out = lax.broadcasted_iota(jnp.int32, (4 * PAD, 4 * PIECE), 1)
    r_in = lax.broadcasted_iota(jnp.int32, (4 * PAD, 4 * PIECE), 0)
    quarter = lax.div(r_out, PIECE)
    pick = (r_in == quarter * PAD + (r_out - quarter * PIECE)).astype(jnp.bfloat16)

    for col in range(NX):
        parts = []
        for pair in range(NY // 2):
            four = [spad[2 * col + low, row] for row in (2 * pair, 2 * pair + 1) for low in (0, 1)]
            padded = jnp.concatenate(four, axis=0)
            parts.append(lax.dot_general(pick, padded, (((0,), (0,)), ((), ())), preferred_element_type=F32))
        swt[576 * col : 576 * (col + 1), :] = jnp.concatenate(parts, axis=0).astype(jnp.bfloat16)
    swr[...] = swt[...].T

    def wait_labels(k, _):
        other = lax.rem(me + k, 8)
        remote(labs.at[other], labs.at[other], lab_s.at[k], lab_r.at[other], sib).wait_recv()
        return 0

    lax.fori_loop(1, 8, wait_labels, 0)
    for copy in own_copies:
        copy.wait()
    for h in (0, 1):
        for a in (0, 1):
            from_sib(0, x, h, a).wait_recv()

    entry = lax.broadcasted_iota(jnp.int32, (SLAB, 2 * ROWS), 0) + me * SLAB

    def label_row(block, i):
        return jnp.concatenate([labs[2 * block, i : i + 1, :], labs[2 * block + 1, i : i + 1, :]], axis=1)

    def logits(block, sums):
        rows_t = rt[pl.ds(2 * block, 2)].reshape(2 * ROWS, rt.shape[2])
        lt = lax.dot_general(tslab[...], rows_t, NT, preferred_element_type=F32)
        rows_s = rs[pl.ds(2 * block, 2)].reshape(2 * ROWS, rs.shape[2])
        ls = lax.dot_general(swr[...], rows_s, NT, preferred_element_type=F32)
        rst[:, pl.ds(pl.multiple_of(block * 2 * ROWS, 2 * ROWS), 2 * ROWS)] = rows_s.T
        top_t = jnp.max(lt, axis=0, keepdims=True)
        top_s = jnp.max(ls, axis=0, keepdims=True)
        exp_t, exp_s = jnp.exp(lt - top_t), jnp.exp(ls - top_s)
        hit = entry == label_row(block, 0)
        et[block] = exp_t
        es[block] = exp_s
        sums[...] = jnp.concatenate(
            [
                top_t,
                top_s,
                jnp.sum(exp_t, axis=0, keepdims=True),
                jnp.sum(exp_t * (lt - ls), axis=0, keepdims=True),
                jnp.sum(exp_s, axis=0, keepdims=True),
                jnp.sum(jnp.where(hit, ls, 0.0), axis=0, keepdims=True),
                jnp.zeros((2, 2 * ROWS), F32),
            ],
            axis=0,
        )

    logits(x, stats.at[me, x])
    for d in (0, 1):
        for h in (0, 1):
            for a in (0, 1):
                from_sib(1 + d, (xl, xr)[d], h, a).wait_recv()
        logits((xl, xr)[d], stats.at[me, (xl, xr)[d]])
    def early_copy(k, slot):
        return remote(stats.at[slot], stats.at[slot], st_s.at[k], st_r.at[slot], group_dev(lax.rem(me + k, 8)))

    def late_copy(k, slot):
        return remote(late.at[slot], late.at[slot], sl_s.at[k], sl_r.at[slot], group_dev(lax.rem(me + k, 8)))

    def send_early(k, _):
        early_copy(k, me).start()
        return 0

    def send_stats(k, _):
        late_copy(k, me).start()
        return 0

    def wait_stats(k, _):
        other = lax.rem(me + k, 8)
        early_copy(k, me).wait_send()
        early_copy(k, other).wait_recv()
        late_copy(k, other).wait_recv()
        return 0

    lax.fori_loop(1, 8, send_early, 0)
    for a in (0, 1):
        for d in (0, 1):
            came_on(d, a).wait_recv()
            to_sib(3, xo, d, a).start()
    for d in (0, 1):
        for a in (0, 1):
            from_sib(3, xo, d, a).wait_recv()
    logits(xo, late.at[me])

    lax.fori_loop(1, 8, send_stats, 0)
    lax.fori_loop(1, 8, wait_stats, 0)
    for sender in range(8):
        stats[sender, (sender // 2 + 2) % NX] = late[sender]

    for block in range(NX):
        tops_t, tops_s = stats[:, block, 0, :], stats[:, block, 1, :]
        top_t = jnp.max(tops_t, axis=0, keepdims=True)
        top_s = jnp.max(tops_s, axis=0, keepdims=True)
        scale_t, scale_s = jnp.exp(tops_t - top_t), jnp.exp(tops_s - top_s)
        sum_t = jnp.sum(stats[:, block, 2, :] * scale_t, axis=0, keepdims=True)
        cross = jnp.sum(stats[:, block, 3, :] * scale_t, axis=0, keepdims=True)
        sum_s = jnp.sum(stats[:, block, 4, :] * scale_s, axis=0, keepdims=True)
        target = jnp.sum(stats[:, block, 5, :], axis=0, keepdims=True)
        lse_t, lse_s = top_t + jnp.log(sum_t), top_s + jnp.log(sum_s)
        weight = label_row(block, 1).astype(F32)
        loss = weight * (cross / sum_t - lse_t + lse_s + 0.5 * (lse_s - target))
        losses[2 * block] = loss[:, :ROWS]
        losses[2 * block + 1] = loss[:, ROWS:]
        prob_t = et[block] * (jnp.exp(stats[me, block, 0:1, :] - top_t) / sum_t)
        prob_s = es[block] * (jnp.exp(stats[me, block, 1:2, :] - top_s) / sum_s)
        onehot = (entry == label_row(block, 0)).astype(F32)
        grad = weight * ((prob_s - prob_t) + 0.5 * (prob_s - onehot))
        lg[:, 2 * ROWS * block : 2 * ROWS * (block + 1)] = grad.astype(jnp.bfloat16)
    loss_ref[...] = losses[me]

    half_cols = g.shape[0] // 2 * g.shape[1] * g.shape[2]
    for j in range(2):
        rows_s = rst[half_cols * j : half_cols * (j + 1), :]
        tile = lax.dot_general(rows_s, lg[...], NT, preferred_element_type=F32)
        tile = tile.reshape((2,) + g.shape[1:])
        g[2 * j : 2 * j + 2] = tile
        rest = jnp.zeros((2, NY, TALL - 2 * PIECE, SLAB), F32)
        gb[2 * j : 2 * j + 2] = jnp.concatenate([tile, rest], axis=2).astype(jnp.bfloat16)

    def low16(dz):
        return pl.multiple_of(lax.rem(dz, 2) * 32, 16)

    def sum_copies(k):
        to_y, to_z = lax.rem(y + k, NY), lax.rem(z + k, NZ)
        return (
            remote(
                gb.at[:, to_y, :, pl.ds(0, 128)], yq.at[y], ys_s.at[k], ys_r.at[y], dev(x, to_y, z, c)
            ),
            remote(
                gb.at[lax.div(to_z, 2), :, pl.ds(low16(to_z), WIN16), pl.ds(128, 128)],
                zq.at[z], zq_s.at[k], zq_r.at[z], dev(x, y, to_z, c),
            ),
        )

    def sum_start(k, _):
        for copy in sum_copies(k):
            copy.start()
        return 0

    lax.fori_loop(1, 8, sum_start, 0)
    ya[...] = g[:, y, :, :128]
    za[...] = g[zh, :, pl.ds(pl.multiple_of(zl * 32, 8), WIN), 128:]

    def sum_add(k, _):
        from_y, from_z = lax.rem(y + k, NY), lax.rem(z + k, NZ)
        remote(yq.at[from_y], yq.at[from_y], ys_s.at[k], ys_r.at[from_y], sib).wait_recv()
        ya[...] += yq[from_y].astype(F32)[:, : 2 * PIECE]
        remote(zq.at[from_z], zq.at[from_z], zq_s.at[k], zq_r.at[from_z], sib).wait_recv()
        za[...] += zq[from_z].astype(F32)[:, :WIN]
        return 0

    lax.fori_loop(1, 8, sum_add, 0)

    def part_y(dz):
        return ya.at[lax.div(dz, 2), pl.ds(pl.multiple_of(lax.rem(dz, 2) * 32, 8), WIN)]

    def last_copies(k):
        to_z, to_y = lax.rem(z + k, NZ), lax.rem(y + k, NY)
        return (
            remote(part_y(to_z), y2.at[z], zr_s.at[k], zr_r.at[z], dev(x, y, to_z, c)),
            remote(za.at[to_y], z2.at[y], yr_s.at[k], yr_r.at[y], dev(x, to_y, z, c)),
        )

    def last_start(k, _):
        for copy in last_copies(k):
            copy.start()
        return 0

    def last_wait(k, _):
        from_z, from_y = lax.rem(z + k, NZ), lax.rem(y + k, NY)
        remote(y2.at[from_z], y2.at[from_z], zr_s.at[k], zr_r.at[from_z], sib).wait_recv()
        remote(z2.at[from_y], z2.at[from_y], yr_s.at[k], yr_r.at[from_y], sib).wait_recv()
        return 0

    lax.fori_loop(1, 8, last_start, 0)
    y2[z] = part_y(z)[...]
    z2[y] = za[y]
    lax.fori_loop(1, 8, last_wait, 0)
    ow[...] = jnp.concatenate([jnp.sum(y2[...], axis=0), jnp.sum(z2[...], axis=0)], axis=1)

    @pl.when(away)
    def _():
        copy = remote(ow, ox, o_s, o_r, partner)
        copy.start()
        copy.wait()

    @pl.when(jnp.logical_not(away))
    def _():
        ox[...] = ow[...]

    out_ref[...] = jnp.where(zl == 0, ox[:PIECE], ox[WIN - PIECE :])

    for d in (0, 1):
        for a in (0, 1):
            for h in (0, 1):
                send_own(d, h, a).wait_send()
            pass_on(d, a).wait_send()
    for a in (0, 1):
        for h in (0, 1):
            own_to_sib(h, a).wait_send()
            for n, block in ((1, xl), (2, xr), (3, xo)):
                to_sib(n, block, h, a).wait_send()
    for step in range(4):
        for d in (0, 1):
            for h in (0, 1):
                if step < 3 or h == d:
                    for a in (0, 1):
                        ring_copy(a, d, step, h, False).wait_send()

    def wait_sent(k, _):
        remote(labs.at[me], labs.at[me], lab_s.at[k], lab_r.at[me], sib).wait_send()
        for copy in z_copies(k, False):
            copy.wait_send()
        late_copy(k, me).wait_send()
        for copy in sum_copies(k) + last_copies(k):
            copy.wait_send()
        return 0

    lax.fori_loop(1, 8, wait_sent, 0)


def per_device(teacher_hidden, student_hidden, teacher_head, student_head, targets, row_mask):
    dt, ds = teacher_hidden.shape[1], student_hidden.shape[1]
    bf16 = jnp.bfloat16
    dma = pltpu.SemaphoreType.DMA
    anywhere, vmem = pl.BlockSpec(memory_space=pl.ANY), pl.BlockSpec(memory_space=pltpu.VMEM)
    loss, out = pl.pallas_call(
        kernel,
        out_shape=(jax.ShapeDtypeStruct((1, ROWS), F32), jax.ShapeDtypeStruct((PIECE, SLAB), F32)),
        in_specs=[anywhere, anywhere, anywhere, vmem, vmem, vmem],
        out_specs=(vmem, vmem),
        scratch_shapes=[
            pltpu.VMEM((8, ROWS, dt), bf16),
            pltpu.VMEM((8, ROWS, ds), bf16),
            pltpu.VMEM((PAD, SLAB), bf16),
            pltpu.VMEM((SLAB, dt), bf16),
            pltpu.VMEM((NZ, NY, PAD, SLAB), bf16),
            pltpu.VMEM((ds, SLAB), bf16),
            pltpu.VMEM((SLAB, ds), bf16),
            pltpu.VMEM((ds, 8 * ROWS), bf16),
            pltpu.VMEM((NX, SLAB, 2 * ROWS), F32),
            pltpu.VMEM((NX, SLAB, 2 * ROWS), F32),
            pltpu.VMEM((SLAB, 8 * ROWS), bf16),
            pltpu.VMEM((NX, NY, 2 * PIECE, SLAB), F32),
            pltpu.VMEM((NX, NY, TALL, SLAB), bf16),
            pltpu.VMEM((NY, NX, TALL, 128), bf16),
            pltpu.VMEM((NZ, NY, WIN16, 128), bf16),
            pltpu.VMEM((NX, 2 * PIECE, 128), F32),
            pltpu.VMEM((NY, WIN, 128), F32),
            pltpu.VMEM((NZ, WIN, 128), F32),
            pltpu.VMEM((NY, WIN, 128), F32),
            pltpu.VMEM((WIN, SLAB), F32),
            pltpu.VMEM((WIN, SLAB), F32),
            pltpu.VMEM((8, 8, ROWS), jnp.int32),
            pltpu.VMEM((8, NX, 8, 2 * ROWS), F32),
            pltpu.VMEM((8, 8, 2 * ROWS), F32),
            pltpu.VMEM((8, 1, ROWS), F32),
            dma((4,)),
            dma((8,)), dma((8,)),
            dma((2,)), dma((2,)),
            dma((8,)), dma((8,)), dma((8,)), dma((8,)),
            dma((2, 2, 4, 2)), dma((2, 2, 4, 2)),
            dma((2, 2, 2)), dma((2, 2, 2)),
            dma((2, 2)), dma((2, 2)),
            dma((4, 2, 2)), dma((4, 2, 2)),
            dma((8,)), dma((8,)), dma((8,)), dma((8,)),
            dma((8,)), dma((8,)), dma((8,)), dma((8,)),
            dma((8,)), dma((8,)), dma((8,)), dma((8,)),
            dma, dma,
        ],
        compiler_params=pltpu.CompilerParams(
            collective_id=0, has_side_effects=True, vmem_limit_bytes=56 * 1024 * 1024
        ),
        cost_estimate=pl.CostEstimate(flops=4_900_000_000, bytes_accessed=6_000_000, transcendentals=1_000_000),
    )(teacher_hidden, student_hidden, teacher_head, student_head, targets.reshape(1, ROWS), row_mask.reshape(1, ROWS))
    return loss.reshape(ROWS), out


def solution(mesh):
    in_specs = (
        P(("tok", "voc"), None),
        P(("tok", "voc"), None),
        P("voc", None),
        P("tok", "voc"),
        P(("tok", "voc")),
        P(("tok", "voc")),
    )
    out_specs = (P(("tok", "voc")), P("tok", "voc"))
    return jax.shard_map(
        per_device, mesh=mesh, in_specs=in_specs, out_specs=out_specs, check_vma=False
    )
```

```python
import jax
import jax.numpy as jnp
from jax import lax
from jax.experimental import pallas as pl
from jax.experimental.pallas import tpu as pltpu
from jax.sharding import PartitionSpec as P

NX, NY, NZ = 4, 8, 8
ROWS = 128
PART = ROWS // 4
BLOCK = 8 * PART
SLAB = 256
PIECE = 36
PAD = 48
WIN = 40
CHUNK = 8 * PIECE
MESH = pl.DeviceIdType.MESH
F32 = jnp.float32
NT = (((1,), (1,)), ((), ()))


def remote(src, dst, send, recv, device):
    return pltpu.make_async_remote_copy(
        src_ref=src, dst_ref=dst, send_sem=send, recv_sem=recv, device_id=device, device_id_type=MESH
    )


def kernel(
    th, sh, tw, sw, target_in, mask_in, loss_ref, out_ref,
    rt, rs, piece_ref, tslab, spad, swt, swr, rst, et, es, lg, gpf, gpb, gzf, gzb, yq, zq, ya, za, y2, z2, ow, ox, labs, stats,
    loc_sem, lab_s, lab_r, tr_s, tr_r, zs_s, zs_r, h_s, h_r,
    x_s, x_r, b_s, b_r, bo_s, bo_r, st_s, st_r, ys_s, ys_r, zq_s, zq_r, yr_s, yr_r, zr_s, zr_r, o_s, o_r,
):
    tok, voc = lax.axis_index("tok"), lax.axis_index("voc")
    x, y, zl = lax.div(tok, 16), lax.rem(lax.div(tok, 2), NY), lax.rem(tok, 2)
    zh, c = lax.div(voc, 2), lax.rem(voc, 2)
    z = zh * 2 + zl
    xh, xl, yh, yl = lax.div(x, 2), lax.rem(x, 2), lax.div(y, 2), lax.rem(y, 2)
    slab = xl * 2 + yl
    me = slab * 2 + c
    p = xh * 4 + yh

    def dev(dx, dy, dz, dc):
        return ((dx * NY + dy) * 2 + lax.rem(dz, 2), lax.div(dz, 2) * 2 + dc)

    def p_dev(dp):
        return dev(lax.div(dp, 4) * 2 + xl, lax.rem(dp, 4) * 2 + yl, z, c)

    def square_xy(q, to_xl, to_yl):
        tx, ty = q // 2, q % 2
        step_x = lax.rem(xl + to_xl, 2) * (1 + 2 * lax.rem(xl + tx, 2))
        step_y = lax.rem(yl + to_yl, 2) * (1 + 6 * lax.rem(yl + ty, 2))
        return lax.rem(x + step_x, NX), lax.rem(y + step_y, NY)

    def group_dev(q, i):
        dx, dy = square_xy(q, lax.div(i, 4), lax.rem(lax.div(i, 2), 2))
        return dev(dx, dy, z, lax.rem(i, 2))

    def other_chip(m):
        return lax.rem(xl + m // 2, 2), lax.rem(yl + m % 2, 2)

    sib = dev(x, y, z, 1 - c)
    z_up, z_down = dev(x, y, lax.rem(z + 1, NZ), c), dev(x, y, lax.rem(z + NZ - 1, NZ), c)
    partner = dev(xh * 2 + lax.div(zh, 2), yh * 2 + lax.rem(zh, 2), slab * 2 + zl, c)
    away = slab != zh

    barrier = pltpu.get_barrier_semaphore()

    def hail(device):
        pl.semaphore_signal(barrier, inc=1, device_id=device, device_id_type=MESH)

    @pl.when(away)
    def _():
        hail(partner)

    hail(sib)
    for dx in (0, 1, NX - 1):
        for dy in (0, 1, NY - 1):
            if dx or dy:
                for dc in (0, 1):
                    hail(dev(lax.rem(x + dx, NX), lax.rem(y + dy, NY), z, dc))

    def greet(k, _):
        hail(dev(x, y, lax.rem(z + k, NZ), c))
        hail(p_dev(lax.rem(p + k, 8)))
        return 0

    lax.fori_loop(1, 8, greet, 0)

    pairs = ((sh, rs), (th, rt))
    own_copies = [pltpu.make_async_copy(pairs[a][0], pairs[a][1].at[:, me], loc_sem.at[a]) for a in (0, 1)]
    for copy in own_copies:
        copy.start()
    piece_ref[...] = jnp.concatenate([sw[...], jnp.zeros((PAD - PIECE, SLAB), sw.dtype)], axis=0)
    own_labels = jnp.concatenate([target_in[...], mask_in[...], jnp.zeros((6, ROWS), jnp.int32)], axis=0)
    for q in range(4):
        labs[q, me] = own_labels

    @pl.when(away)
    def _():
        pl.semaphore_wait(barrier, 32)

    @pl.when(jnp.logical_not(away))
    def _():
        pl.semaphore_wait(barrier, 31)

    def head_rows(dz):
        return pl.ds(pl.multiple_of(dz * 32, 32), 32)

    def turn(dz):
        return tw.at[head_rows(dz)], tslab.at[head_rows(dz)], spad.at[dz, p]

    def turn_copies():
        src_t, dst_t, dst_s = turn(slab * 2 + zl)
        return (
            remote(src_t, dst_t, tr_s.at[0], tr_r.at[0], partner),
            remote(piece_ref, dst_s, tr_s.at[1], tr_r.at[1], partner),
        )

    def turn_local():
        src_t, dst_t, dst_s = turn(slab * 2 + zl)
        return (
            pltpu.make_async_copy(src_t, dst_t, loc_sem.at[2]),
            pltpu.make_async_copy(piece_ref, dst_s, loc_sem.at[3]),
        )

    @pl.when(away)
    def _():
        for copy in turn_copies():
            copy.start()

    @pl.when(jnp.logical_not(away))
    def _():
        for copy in turn_local():
            copy.start()

    def send_rows(q, m, a):
        dx, dy = square_xy(q, *other_chip(m))
        src, dst = pairs[a]
        return remote(src.at[q], dst.at[q, me], x_s.at[q, m - 1, a], x_r.at[q, m - 1, a], dev(dx, dy, z, c))

    def slot_of(m, core):
        ox_, oy_ = other_chip(m)
        return (ox_ * 2 + oy_) * 2 + core

    def came_rows(q, m, a):
        part = pairs[a][1].at[q, slot_of(m, c)]
        return remote(part, part, x_s.at[q, m - 1, a], x_r.at[q, m - 1, a], sib)

    def to_sib(q, m, a):
        part = pairs[a][1].at[q, slot_of(m, c)]
        return remote(part, part, b_s.at[q, m - 1, a], b_r.at[q, m - 1, a], sib)

    def from_sib(q, m, a):
        part = pairs[a][1].at[q, slot_of(m, 1 - c)]
        return remote(part, part, b_s.at[q, m - 1, a], b_r.at[q, m - 1, a], sib)

    def own_to_sib(a):
        return remote(pairs[a][0], pairs[a][1].at[:, me], bo_s.at[a], bo_r.at[a], sib)

    def own_from_sib(a):
        part = pairs[a][1].at[:, slab * 2 + 1 - c]
        return remote(part, part, bo_s.at[a], bo_r.at[a], sib)

    for q in range(4):
        for m in (1, 2, 3):
            for a in (0, 1):
                send_rows(q, m, a).start()
    for a in (0, 1):
        own_to_sib(a).start()

    def take_rows(q):
        for a in (0, 1):
            for m in (1, 2, 3):
                came_rows(q, m, a).wait_recv()
                to_sib(q, m, a).start()

    def label_copy(q, k, slot):
        part = labs.at[q, slot]
        return remote(part, part, lab_s.at[q, k], lab_r.at[q, slot], group_dev(q, lax.rem(me + k, 8)))

    def send_labels(k, _):
        for q in range(4):
            label_copy(q, k, me).start()
        return 0

    lax.fori_loop(1, 8, send_labels, 0)

    @pl.when(away)
    def _():
        for copy in turn_copies():
            copy.wait_send()
        src_t, dst_t, dst_s = turn(z)
        remote(dst_t, dst_t, tr_s.at[0], tr_r.at[0], partner).wait_recv()
        remote(dst_s, dst_s, tr_s.at[1], tr_r.at[1], partner).wait_recv()

    @pl.when(jnp.logical_not(away))
    def _():
        for copy in turn_local():
            copy.wait()

    def p_copy(k, back):
        dp = lax.rem(p + k, 8)
        sp = dp if back else p
        piece = spad.at[z, sp]
        return remote(piece, piece, zs_s.at[k], zs_r.at[sp], p_dev(dp))

    def p_start(k, _):
        p_copy(k, False).start()
        return 0

    def p_wait(k, _):
        p_copy(k, True).wait_recv()
        return 0

    def ring_copy(a, d, step, h, back):
        gap = step + 1 if back else step
        chunk = lax.rem(z + (8 - gap, gap)[d], NZ)
        if a == 0:
            piece = tslab.at[pl.ds(pl.multiple_of(chunk * 32 + 16 * h, 16), 16)]
        else:
            piece = spad.at[chunk, pl.ds(4 * h, 4)]
        return remote(piece, piece, h_s.at[a, d, step, h], h_r.at[a, d, step, h], (z_up, z_down)[d])

    def ring_step(a, step):
        for h in (0, 1):
            for d in (0, 1):
                if 0 < step < 4 or (step == 4 and h == d):
                    ring_copy(a, d, step - 1, h, True).wait_recv()
                if step < 3 or (step == 3 and h == d):
                    ring_copy(a, d, step, h, False).start()

    lax.fori_loop(1, 8, p_start, 0)
    ring_step(0, 0)
    lax.fori_loop(1, 8, p_wait, 0)
    ring_step(1, 0)
    for step in range(1, 5):
        ring_step(0, step)
        take_rows(step - 1)
        ring_step(1, step)

    r_out = lax.broadcasted_iota(jnp.int32, (4 * PAD, 4 * PIECE), 1)
    r_in = lax.broadcasted_iota(jnp.int32, (4 * PAD, 4 * PIECE), 0)
    quarter = lax.div(r_out, PIECE)
    pick = (r_in == quarter * PAD + (r_out - quarter * PIECE)).astype(jnp.bfloat16)

    for col in range(NX):
        parts = []
        for pair in range(NY // 2):
            four = [
                spad[2 * (2 * (col % 2) + odd) + low, 4 * (col // 2) + pair] for odd in (0, 1) for low in (0, 1)
            ]
            padded = jnp.concatenate(four, axis=0)
            parts.append(lax.dot_general(pick, padded, (((0,), (0,)), ((), ())), preferred_element_type=F32))
        swt[576 * col : 576 * (col + 1), :] = jnp.concatenate(parts, axis=0).astype(jnp.bfloat16)
    swr[...] = swt[...].T

    def wait_labels(k, _):
        for q in range(4):
            label_copy(q, k, lax.rem(me + k, 8)).wait_recv()
        return 0

    lax.fori_loop(1, 8, wait_labels, 0)
    for copy in own_copies:
        copy.wait()
    for a in (0, 1):
        own_from_sib(a).wait_recv()

    entry = lax.broadcasted_iota(jnp.int32, (SLAB, BLOCK), 0) + me * SLAB

    def label_row(q, i):
        return jnp.concatenate([labs[q, slot, i : i + 1, PART * q : PART * (q + 1)] for slot in range(8)], axis=1)

    def logits(q):
        rows_t = rt[q].reshape(BLOCK, rt.shape[3])
        lt = lax.dot_general(tslab[...], rows_t, NT, preferred_element_type=F32)
        rows_s = rs[q].reshape(BLOCK, rs.shape[3])
        ls = lax.dot_general(swr[...], rows_s, NT, preferred_element_type=F32)
        rst[:, BLOCK * q : BLOCK * (q + 1)] = rows_s.T
        top_t = jnp.max(lt, axis=0, keepdims=True)
        top_s = jnp.max(ls, axis=0, keepdims=True)
        exp_t, exp_s = jnp.exp(lt - top_t), jnp.exp(ls - top_s)
        hit = entry == label_row(q, 0)
        et[q] = exp_t
        es[q] = exp_s
        stats[q, me] = jnp.concatenate(
            [
                top_t,
                top_s,
                jnp.sum(exp_t, axis=0, keepdims=True),
                jnp.sum(exp_t * (lt - ls), axis=0, keepdims=True),
                jnp.sum(exp_s, axis=0, keepdims=True),
                jnp.sum(jnp.where(hit, ls, 0.0), axis=0, keepdims=True),
                jnp.zeros((2, BLOCK), F32),
            ],
            axis=0,
        )

    def stats_copy(q, k, slot):
        part = stats.at[q, slot]
        return remote(part, part, st_s.at[q, k], st_r.at[q, slot], group_dev(q, lax.rem(me + k, 8)))

    for q in range(4):
        for m in (1, 2, 3):
            for a in (0, 1):
                from_sib(q, m, a).wait_recv()
        logits(q)

        def send_stats(k, _, q=q):
            stats_copy(q, k, me).start()
            return 0

        lax.fori_loop(1, 8, send_stats, 0)

    own_losses = []
    for block in range(4):
        def wait_stats(k, _, q=block):
            stats_copy(q, k, lax.rem(me + k, 8)).wait_recv()
            return 0

        lax.fori_loop(1, 8, wait_stats, 0)
        tops_t, tops_s = stats[block, :, 0, :], stats[block, :, 1, :]
        top_t = jnp.max(tops_t, axis=0, keepdims=True)
        top_s = jnp.max(tops_s, axis=0, keepdims=True)
        scale_t, scale_s = jnp.exp(tops_t - top_t), jnp.exp(tops_s - top_s)
        sum_t = jnp.sum(stats[block, :, 2, :] * scale_t, axis=0, keepdims=True)
        cross = jnp.sum(stats[block, :, 3, :] * scale_t, axis=0, keepdims=True)
        sum_s = jnp.sum(stats[block, :, 4, :] * scale_s, axis=0, keepdims=True)
        target = jnp.sum(stats[block, :, 5, :], axis=0, keepdims=True)
        lse_t, lse_s = top_t + jnp.log(sum_t), top_s + jnp.log(sum_s)
        weight = label_row(block, 1).astype(F32)
        loss = weight * (cross / sum_t - lse_t + lse_s + 0.5 * (lse_s - target))
        mine = jnp.zeros((1, PART), F32)
        for slot in range(8):
            mine = jnp.where(me == slot, loss[:, PART * slot : PART * (slot + 1)], mine)
        own_losses.append(mine)
        prob_t = et[block] * (jnp.exp(stats[block, me, 0:1, :] - top_t) / sum_t)
        prob_s = es[block] * (jnp.exp(stats[block, me, 1:2, :] - top_s) / sum_s)
        onehot = (entry == label_row(block, 0)).astype(F32)
        grad = weight * ((prob_s - prob_t) + 0.5 * (prob_s - onehot))
        lg[:, BLOCK * block : BLOCK * (block + 1)] = grad.astype(jnp.bfloat16)
    loss_ref[...] = jnp.concatenate(own_losses, axis=1)

    half_cols = rst.shape[0] // 2
    for j in range(2):
        tile = lax.dot_general(
            rst[half_cols * j : half_cols * (j + 1), :], lg[...], NT, preferred_element_type=F32
        ).reshape(2, NY, 2 * PIECE, SLAB)
        for i in range(4):
            part = jnp.concatenate([tile[a, 2 * i + b, :, :128] for a in (0, 1) for b in (0, 1)], axis=0)
            gpf[4 * j + i] = part
            gpb[4 * j + i] = part.astype(jnp.bfloat16)
        for dz in range(NZ):
            a, b, low = dz // 4, dz // 2 % 2, dz % 2 * PIECE
            part = jnp.concatenate([tile[a, 2 * i + b, low : low + PIECE, 128:] for i in range(4)], axis=0)
            gzf[dz, 4 * PIECE * j : 4 * PIECE * (j + 1)] = part
            gzb[dz, 4 * PIECE * j : 4 * PIECE * (j + 1)] = part.astype(jnp.bfloat16)

    def sum_copies(k):
        to_p, to_z = lax.rem(p + k, 8), lax.rem(z + k, NZ)
        return (
            remote(gpb.at[to_p], yq.at[p], ys_s.at[k], ys_r.at[p], p_dev(to_p)),
            remote(gzb.at[to_z], zq.at[z], zq_s.at[k], zq_r.at[z], dev(x, y, to_z, c)),
        )

    def sum_start(k, _):
        for copy in sum_copies(k):
            copy.start()
        return 0

    lax.fori_loop(1, 8, sum_start, 0)
    ya[...] = gpf[p]
    za[...] = gzf[z]

    def sum_add(k, _):
        from_p, from_z = lax.rem(p + k, 8), lax.rem(z + k, NZ)
        remote(yq.at[from_p], yq.at[from_p], ys_s.at[k], ys_r.at[from_p], sib).wait_recv()
        ya[...] += yq[from_p].astype(F32)
        remote(zq.at[from_z], zq.at[from_z], zq_s.at[k], zq_r.at[from_z], sib).wait_recv()
        za[...] += zq[from_z].astype(F32)
        return 0

    lax.fori_loop(1, 8, sum_add, 0)

    def window(ref, i):
        start = lax.div(i, 2) * 2 * PIECE + lax.rem(i, 2) * 32
        return ref.at[pl.ds(pl.multiple_of(start, 8), WIN)]

    def last_copies(k):
        to_z, to_p = lax.rem(z + k, NZ), lax.rem(p + k, 8)
        return (
            remote(window(ya, to_z), y2.at[z], zr_s.at[k], zr_r.at[z], dev(x, y, to_z, c)),
            remote(window(za, to_p), z2.at[p], yr_s.at[k], yr_r.at[p], p_dev(to_p)),
        )

    def last_start(k, _):
        for copy in last_copies(k):
            copy.start()
        return 0

    def last_wait(k, _):
        from_z, from_p = lax.rem(z + k, NZ), lax.rem(p + k, 8)
        remote(y2.at[from_z], y2.at[from_z], zr_s.at[k], zr_r.at[from_z], sib).wait_recv()
        remote(z2.at[from_p], z2.at[from_p], yr_s.at[k], yr_r.at[from_p], sib).wait_recv()
        return 0

    lax.fori_loop(1, 8, last_start, 0)
    y2[z] = window(ya, z)[...]
    z2[p] = window(za, p)[...]
    lax.fori_loop(1, 8, last_wait, 0)

    def piece_of(ref, odd):
        total = jnp.sum(ref[...], axis=0)
        return jnp.where(odd == 0, total[:PIECE], total[WIN - PIECE :])

    ow[:PIECE] = jnp.concatenate([piece_of(y2, zl), piece_of(z2, lax.rem(p, 2))], axis=1)
    ow[PIECE:] = jnp.zeros((WIN - PIECE, SLAB), F32)

    @pl.when(away)
    def _():
        copy = remote(ow, ox, o_s, o_r, partner)
        copy.start()
        copy.wait()

    @pl.when(jnp.logical_not(away))
    def _():
        ox[...] = ow[...]

    out_ref[...] = ox[:PIECE]

    for a in (0, 1):
        own_to_sib(a).wait_send()
        for q in range(4):
            for m in (1, 2, 3):
                send_rows(q, m, a).wait_send()
                to_sib(q, m, a).wait_send()
    for step in range(4):
        for d in (0, 1):
            for h in (0, 1):
                if step < 3 or h == d:
                    for a in (0, 1):
                        ring_copy(a, d, step, h, False).wait_send()

    def wait_sent(k, _):
        p_copy(k, False).wait_send()
        for q in range(4):
            label_copy(q, k, me).wait_send()
            stats_copy(q, k, me).wait_send()
        for copy in sum_copies(k) + last_copies(k):
            copy.wait_send()
        return 0

    lax.fori_loop(1, 8, wait_sent, 0)


def per_device(teacher_hidden, student_hidden, teacher_head, student_head, targets, row_mask):
    dt, ds = teacher_hidden.shape[1], student_hidden.shape[1]
    rows_t, rows_s = teacher_hidden.reshape(4, PART, dt), student_hidden.reshape(4, PART, ds)
    bf16 = jnp.bfloat16
    dma = pltpu.SemaphoreType.DMA
    anywhere, vmem = pl.BlockSpec(memory_space=pl.ANY), pl.BlockSpec(memory_space=pltpu.VMEM)
    loss, out = pl.pallas_call(
        kernel,
        out_shape=(jax.ShapeDtypeStruct((1, ROWS), F32), jax.ShapeDtypeStruct((PIECE, SLAB), F32)),
        in_specs=[anywhere, anywhere, anywhere, vmem, vmem, vmem],
        out_specs=(vmem, vmem),
        scratch_shapes=[
            pltpu.VMEM((4, 8, PART, dt), bf16),
            pltpu.VMEM((4, 8, PART, ds), bf16),
            pltpu.VMEM((PAD, SLAB), bf16),
            pltpu.VMEM((SLAB, dt), bf16),
            pltpu.VMEM((NZ, NY, PAD, SLAB), bf16),
            pltpu.VMEM((ds, SLAB), bf16),
            pltpu.VMEM((SLAB, ds), bf16),
            pltpu.VMEM((ds, 8 * ROWS), bf16),
            pltpu.VMEM((4, SLAB, BLOCK), F32),
            pltpu.VMEM((4, SLAB, BLOCK), F32),
            pltpu.VMEM((SLAB, 4 * BLOCK), bf16),
            pltpu.VMEM((8, CHUNK, 128), F32),
            pltpu.VMEM((8, CHUNK, 128), bf16),
            pltpu.VMEM((NZ, CHUNK, 128), F32),
            pltpu.VMEM((NZ, CHUNK, 128), bf16),
            pltpu.VMEM((8, CHUNK, 128), bf16),
            pltpu.VMEM((NZ, CHUNK, 128), bf16),
            pltpu.VMEM((CHUNK, 128), F32),
            pltpu.VMEM((CHUNK, 128), F32),
            pltpu.VMEM((NZ, WIN, 128), F32),
            pltpu.VMEM((NY, WIN, 128), F32),
            pltpu.VMEM((WIN, SLAB), F32),
            pltpu.VMEM((WIN, SLAB), F32),
            pltpu.VMEM((4, 8, 8, ROWS), jnp.int32),
            pltpu.VMEM((4, 8, 8, BLOCK), F32),
            dma((4,)),
            dma((4, 8)), dma((4, 8)),
            dma((2,)), dma((2,)),
            dma((8,)), dma((8,)),
            dma((2, 2, 4, 2)), dma((2, 2, 4, 2)),
            dma((4, 3, 2)), dma((4, 3, 2)), dma((4, 3, 2)), dma((4, 3, 2)),
            dma((2,)), dma((2,)),
            dma((4, 8)), dma((4, 8)),
            dma((8,)), dma((8,)), dma((8,)), dma((8,)),
            dma((8,)), dma((8,)), dma((8,)), dma((8,)),
            dma, dma,
        ],
        compiler_params=pltpu.CompilerParams(
            collective_id=0, has_side_effects=True, vmem_limit_bytes=56 * 1024 * 1024
        ),
        cost_estimate=pl.CostEstimate(flops=4_900_000_000, bytes_accessed=6_000_000, transcendentals=1_000_000),
    )(rows_t, rows_s, teacher_head, student_head, targets.reshape(1, ROWS), row_mask.reshape(1, ROWS))
    return loss.reshape(ROWS), out


def solution(mesh):
    in_specs = (
        P(("tok", "voc"), None),
        P(("tok", "voc"), None),
        P("voc", None),
        P("tok", "voc"),
        P(("tok", "voc")),
        P(("tok", "voc")),
    )
    out_specs = (P(("tok", "voc")), P("tok", "voc"))
    return jax.shard_map(
        per_device, mesh=mesh, in_specs=in_specs, out_specs=out_specs, check_vma=False
    )
```

```python
import jax
import jax.numpy as jnp
from jax import lax
from jax.experimental import pallas as pl
from jax.experimental.pallas import tpu as pltpu
from jax.sharding import PartitionSpec as P

NX, NY, NZ = 4, 8, 8
ROWS = 128
HALF = ROWS // 2
SLAB = 256
PIECE = 36
PAD = 48
WIN = 40
CHUNK = 8 * PIECE
MESH = pl.DeviceIdType.MESH
F32 = jnp.float32
NT = (((1,), (1,)), ((), ()))


def remote(src, dst, send, recv, device):
    return pltpu.make_async_remote_copy(
        src_ref=src, dst_ref=dst, send_sem=send, recv_sem=recv, device_id=device, device_id_type=MESH
    )


def kernel(
    th, sh, tw, sw, target_in, mask_in, loss_ref, out_ref,
    rt, rs, piece_ref, tslab, spad, swt, swr, rst, et, es, lg, gyf, gyb, gzf, gzb, yq, zq, ya, za, y2, z2, ow, ox, labs, stats, late, losses,
    loc_sem, lab_s, lab_r, tr_s, tr_r, zt_s, zt_r, zs_s, zs_r, h_s, h_r,
    x_s, x_r, f_s, f_r, b_s, b_r, st_s, st_r, sl_s, sl_r, ys_s, ys_r, zq_s, zq_r, yr_s, yr_r, zr_s, zr_r, o_s, o_r,
):
    tok, voc = lax.axis_index("tok"), lax.axis_index("voc")
    x, y, zl = lax.div(tok, 16), lax.rem(lax.div(tok, 2), NY), lax.rem(tok, 2)
    zh, c = lax.div(voc, 2), lax.rem(voc, 2)
    z = zh * 2 + zl
    me = x * 2 + c

    def dev(dx, dy, dz, dc):
        return ((dx * NY + dy) * 2 + lax.rem(dz, 2), lax.div(dz, 2) * 2 + dc)

    def group_dev(i):
        return dev(lax.div(i, 2), y, z, lax.rem(i, 2))

    xr, xl, xo = lax.rem(x + 1, NX), lax.rem(x + 3, NX), lax.rem(x + 2, NX)
    right, left, sib = dev(xr, y, z, c), dev(xl, y, z, c), dev(x, y, z, 1 - c)
    up, down = dev(x, lax.rem(y + 1, NY), z, c), dev(x, lax.rem(y + NY - 1, NY), z, c)
    z_up, z_down = dev(x, y, lax.rem(z + 1, NZ), c), dev(x, y, lax.rem(z + NZ - 1, NZ), c)
    partner = dev(zh, y, x * 2 + zl, c)
    away = x != zh

    barrier = pltpu.get_barrier_semaphore()

    def greet(k, _):
        pl.semaphore_signal(barrier, inc=1, device_id=group_dev(lax.rem(me + k, 8)), device_id_type=MESH)
        pl.semaphore_signal(barrier, inc=1, device_id=dev(x, y, lax.rem(z + k, NZ), c), device_id_type=MESH)
        pl.semaphore_signal(barrier, inc=1, device_id=dev(x, lax.rem(y + k, NY), z, c), device_id_type=MESH)
        return 0

    lax.fori_loop(1, 8, greet, 0)

    @pl.when(away)
    def _():
        pl.semaphore_signal(barrier, inc=1, device_id=partner, device_id_type=MESH)

    own_copies = [pltpu.make_async_copy(ref, dst.at[me], loc_sem.at[a]) for a, (ref, dst) in enumerate(((sh, rs), (th, rt)))]
    for copy in own_copies:
        copy.start()
    piece_ref[...] = jnp.concatenate([sw[...], jnp.zeros((PAD - PIECE, SLAB), sw.dtype)], axis=0)
    stats[me] = jnp.zeros(stats.shape[1:], F32)
    labs[me] = jnp.concatenate([target_in[...], mask_in[...], jnp.zeros((6, ROWS), jnp.int32)], axis=0)

    @pl.when(away)
    def _():
        pl.semaphore_wait(barrier, 22)

    @pl.when(jnp.logical_not(away))
    def _():
        pl.semaphore_wait(barrier, 21)

    t_row = pl.multiple_of(y * 32 + zl * 16, 16)

    def t_piece(ref, col):
        return ref.at[pl.ds(t_row, 16), pl.ds(pl.multiple_of(col * 1152, 128), 1152)]

    def turn(dst_col):
        src_t, dst_t = t_piece(tw, x), t_piece(tslab, dst_col)
        dst_s = spad.at[dst_col * 2 + zl, y]
        return src_t, dst_t, dst_s

    def turn_copies():
        src_t, dst_t, dst_s = turn(x)
        return (
            remote(src_t, dst_t, tr_s.at[0], tr_r.at[0], partner),
            remote(piece_ref, dst_s, tr_s.at[1], tr_r.at[1], partner),
        )

    def turn_local():
        src_t, dst_t, dst_s = turn(x)
        return (
            pltpu.make_async_copy(src_t, dst_t, loc_sem.at[2]),
            pltpu.make_async_copy(piece_ref, dst_s, loc_sem.at[3]),
        )

    @pl.when(away)
    def _():
        for copy in turn_copies():
            copy.start()

    @pl.when(jnp.logical_not(away))
    def _():
        for copy in turn_local():
            copy.start()

    def half(ref, block, h):
        return ref.at[block, pl.ds(h * HALF, HALF)]

    pairs = ((sh, rs), (th, rt))

    def send_own(d, h, a):
        src, dst = pairs[a]
        return remote(
            src.at[pl.ds(h * HALF, HALF)], half(dst, me, h), x_s.at[d, h, a], x_r.at[d, h, a], (right, left)[d]
        )

    def came_own(d, h, a):
        block = (xl, xr)[d] * 2 + c
        piece = half(pairs[a][1], block, h)
        return remote(piece, piece, x_s.at[d, h, a], x_r.at[d, h, a], (right, left)[d])

    def pass_on(d, a):
        block = (xl, xr)[d] * 2 + c
        piece = half(pairs[a][1], block, d)
        return remote(piece, piece, f_s.at[d, a], f_r.at[d, a], (right, left)[d])

    def came_on(d, a):
        piece = half(pairs[a][1], xo * 2 + c, d)
        return remote(piece, piece, f_s.at[d, a], f_r.at[d, a], (right, left)[d])

    def to_sib(n, block, h, a):
        piece = half(pairs[a][1], block * 2 + c, h)
        return remote(piece, piece, b_s.at[n, h, a], b_r.at[n, h, a], sib)

    def from_sib(n, block, h, a):
        piece = half(pairs[a][1], block * 2 + 1 - c, h)
        return remote(piece, piece, b_s.at[n, h, a], b_r.at[n, h, a], sib)

    def own_to_sib(h, a):
        src, dst = pairs[a]
        return remote(src.at[pl.ds(h * HALF, HALF)], half(dst, me, h), b_s.at[0, h, a], b_r.at[0, h, a], sib)

    for first in (0, 1):
        for a in (0, 1):
            send_own(0, first, a).start()
            send_own(1, 1 - first, a).start()
    for h in (0, 1):
        for a in (0, 1):
            own_to_sib(h, a).start()

    def send_labels(k, _):
        to = lax.rem(me + k, 8)
        remote(labs.at[me], labs.at[me], lab_s.at[k], lab_r.at[me], group_dev(to)).start()
        return 0

    lax.fori_loop(1, 8, send_labels, 0)

    @pl.when(away)
    def _():
        for copy in turn_copies():
            copy.wait_send()
        src_t, dst_t, dst_s = turn(zh)
        remote(dst_t, dst_t, tr_s.at[0], tr_r.at[0], partner).wait_recv()
        remote(dst_s, dst_s, tr_s.at[1], tr_r.at[1], partner).wait_recv()

    @pl.when(jnp.logical_not(away))
    def _():
        for copy in turn_local():
            copy.wait()

    def z_piece(dz):
        rows = pl.ds(pl.multiple_of(y * 32 + lax.rem(dz, 2) * 16, 16), 16)
        return tslab.at[rows, pl.ds(pl.multiple_of(lax.div(dz, 2) * 1152, 128), 1152)]

    def z_copies(k, back):
        dz, dy = lax.rem(z + k, NZ), lax.rem(y + k, NY)
        sz, sy = (dz, dy) if back else (z, y)
        t, s = z_piece(sz), spad.at[z, sy]
        return (
            remote(t, t, zt_s.at[k], zt_r.at[sz], dev(x, y, dz, c)),
            remote(s, s, zs_s.at[k], zs_r.at[sy], dev(x, dy, z, c)),
        )

    def z_start(k, _):
        for copy in z_copies(k, False):
            copy.start()
        return 0

    def z_wait(k, _):
        for copy in z_copies(k, True):
            copy.wait_recv()
        return 0

    lax.fori_loop(1, NZ, z_start, 0)
    lax.fori_loop(1, NZ, z_wait, 0)

    def ring_copy(a, d, step, h, back):
        gap = step + 1 if back else step
        move = (8 - gap, gap)[d]
        if a == 0:
            chunk = lax.rem(y + move, NY)
            piece = tslab.at[pl.ds(pl.multiple_of(chunk * 32 + 16 * h, 16), 16)]
        else:
            piece = spad.at[lax.rem(z + move, NZ), pl.ds(4 * h, 4)]
        to = ((up, down), (z_up, z_down))[a][d]
        return remote(piece, piece, h_s.at[a, d, step, h], h_r.at[a, d, step, h], to)

    def ring_step(step):
        for h in (0, 1):
            for d in (0, 1):
                for a in (0, 1):
                    if 0 < step < 4 or (step == 4 and h == d):
                        ring_copy(a, d, step - 1, h, True).wait_recv()
                    if step < 3 or (step == 3 and h == d):
                        ring_copy(a, d, step, h, False).start()

    ring_step(0)
    ring_step(1)
    for a in (0, 1):
        for d in (0, 1):
            came_own(d, d, a).wait_recv()
            pass_on(d, a).start()
            to_sib(1 + d, (xl, xr)[d], d, a).start()
    ring_step(2)
    ring_step(3)
    for a in (0, 1):
        for d in (0, 1):
            came_own(d, 1 - d, a).wait_recv()
            to_sib(1 + d, (xl, xr)[d], 1 - d, a).start()
    ring_step(4)

    r_out = lax.broadcasted_iota(jnp.int32, (4 * PAD, 4 * PIECE), 1)
    r_in = lax.broadcasted_iota(jnp.int32, (4 * PAD, 4 * PIECE), 0)
    quarter = lax.div(r_out, PIECE)
    pick = (r_in == quarter * PAD + (r_out - quarter * PIECE)).astype(jnp.bfloat16)

    for col in range(NX):
        parts = []
        for pair in range(NY // 2):
            four = [spad[2 * col + low, row] for row in (2 * pair, 2 * pair + 1) for low in (0, 1)]
            padded = jnp.concatenate(four, axis=0)
            parts.append(lax.dot_general(pick, padded, (((0,), (0,)), ((), ())), preferred_element_type=F32))
        swt[576 * col : 576 * (col + 1), :] = jnp.concatenate(parts, axis=0).astype(jnp.bfloat16)
    swr[...] = swt[...].T

    def wait_labels(k, _):
        other = lax.rem(me + k, 8)
        remote(labs.at[other], labs.at[other], lab_s.at[k], lab_r.at[other], sib).wait_recv()
        return 0

    lax.fori_loop(1, 8, wait_labels, 0)
    for copy in own_copies:
        copy.wait()
    for h in (0, 1):
        for a in (0, 1):
            from_sib(0, x, h, a).wait_recv()

    entry = lax.broadcasted_iota(jnp.int32, (SLAB, 2 * ROWS), 0) + me * SLAB

    def label_row(block, i):
        return jnp.concatenate([labs[2 * block, i : i + 1, :], labs[2 * block + 1, i : i + 1, :]], axis=1)

    def logits(block, sums):
        rows_t = rt[pl.ds(2 * block, 2)].reshape(2 * ROWS, rt.shape[2])
        lt = lax.dot_general(tslab[...], rows_t, NT, preferred_element_type=F32)
        rows_s = rs[pl.ds(2 * block, 2)].reshape(2 * ROWS, rs.shape[2])
        ls = lax.dot_general(swr[...], rows_s, NT, preferred_element_type=F32)
        rst[:, pl.ds(pl.multiple_of(block * 2 * ROWS, 2 * ROWS), 2 * ROWS)] = rows_s.T
        top_t = jnp.max(lt, axis=0, keepdims=True)
        top_s = jnp.max(ls, axis=0, keepdims=True)
        exp_t, exp_s = jnp.exp(lt - top_t), jnp.exp(ls - top_s)
        hit = entry == label_row(block, 0)
        et[block] = exp_t
        es[block] = exp_s
        sums[...] = jnp.concatenate(
            [
                top_t,
                top_s,
                jnp.sum(exp_t, axis=0, keepdims=True),
                jnp.sum(exp_t * (lt - ls), axis=0, keepdims=True),
                jnp.sum(exp_s, axis=0, keepdims=True),
                jnp.sum(jnp.where(hit, ls, 0.0), axis=0, keepdims=True),
                jnp.zeros((2, 2 * ROWS), F32),
            ],
            axis=0,
        )

    logits(x, stats.at[me, x])
    for d in (0, 1):
        for h in (0, 1):
            for a in (0, 1):
                from_sib(1 + d, (xl, xr)[d], h, a).wait_recv()
        logits((xl, xr)[d], stats.at[me, (xl, xr)[d]])
    def early_copy(k, slot):
        return remote(stats.at[slot], stats.at[slot], st_s.at[k], st_r.at[slot], group_dev(lax.rem(me + k, 8)))

    def late_copy(k, slot):
        return remote(late.at[slot], late.at[slot], sl_s.at[k], sl_r.at[slot], group_dev(lax.rem(me + k, 8)))

    def send_early(k, _):
        early_copy(k, me).start()
        return 0

    def send_stats(k, _):
        late_copy(k, me).start()
        return 0

    def wait_stats(k, _):
        other = lax.rem(me + k, 8)
        early_copy(k, me).wait_send()
        early_copy(k, other).wait_recv()
        late_copy(k, other).wait_recv()
        return 0

    lax.fori_loop(1, 8, send_early, 0)
    for a in (0, 1):
        for d in (0, 1):
            came_on(d, a).wait_recv()
            to_sib(3, xo, d, a).start()
    for d in (0, 1):
        for a in (0, 1):
            from_sib(3, xo, d, a).wait_recv()
    logits(xo, late.at[me])

    lax.fori_loop(1, 8, send_stats, 0)
    lax.fori_loop(1, 8, wait_stats, 0)
    for sender in range(8):
        stats[sender, (sender // 2 + 2) % NX] = late[sender]

    for block in range(NX):
        tops_t, tops_s = stats[:, block, 0, :], stats[:, block, 1, :]
        top_t = jnp.max(tops_t, axis=0, keepdims=True)
        top_s = jnp.max(tops_s, axis=0, keepdims=True)
        scale_t, scale_s = jnp.exp(tops_t - top_t), jnp.exp(tops_s - top_s)
        sum_t = jnp.sum(stats[:, block, 2, :] * scale_t, axis=0, keepdims=True)
        cross = jnp.sum(stats[:, block, 3, :] * scale_t, axis=0, keepdims=True)
        sum_s = jnp.sum(stats[:, block, 4, :] * scale_s, axis=0, keepdims=True)
        target = jnp.sum(stats[:, block, 5, :], axis=0, keepdims=True)
        lse_t, lse_s = top_t + jnp.log(sum_t), top_s + jnp.log(sum_s)
        weight = label_row(block, 1).astype(F32)
        loss = weight * (cross / sum_t - lse_t + lse_s + 0.5 * (lse_s - target))
        losses[2 * block] = loss[:, :ROWS]
        losses[2 * block + 1] = loss[:, ROWS:]
        prob_t = et[block] * (jnp.exp(stats[me, block, 0:1, :] - top_t) / sum_t)
        prob_s = es[block] * (jnp.exp(stats[me, block, 1:2, :] - top_s) / sum_s)
        onehot = (entry == label_row(block, 0)).astype(F32)
        grad = weight * ((prob_s - prob_t) + 0.5 * (prob_s - onehot))
        lg[:, 2 * ROWS * block : 2 * ROWS * (block + 1)] = grad.astype(jnp.bfloat16)
    loss_ref[...] = losses[me]

    half_cols = rst.shape[0] // 2
    for j in range(2):
        tile = lax.dot_general(
            rst[half_cols * j : half_cols * (j + 1), :], lg[...], NT, preferred_element_type=F32
        ).reshape(2, NY, 2 * PIECE, SLAB)
        for i in range(NY):
            part = jnp.concatenate([tile[0, i, :, :128], tile[1, i, :, :128]], axis=0)
            gyf[i, 4 * PIECE * j : 4 * PIECE * (j + 1)] = part
            gyb[i, 4 * PIECE * j : 4 * PIECE * (j + 1)] = part.astype(jnp.bfloat16)
        for a in (0, 1):
            for low in (0, 1):
                part = jnp.concatenate([tile[a, i, low * PIECE : (low + 1) * PIECE, 128:] for i in range(NY)], axis=0)
                gzf[4 * j + 2 * a + low] = part
                gzb[4 * j + 2 * a + low] = part.astype(jnp.bfloat16)

    def sum_copies(k):
        to_y, to_z = lax.rem(y + k, NY), lax.rem(z + k, NZ)
        return (
            remote(gyb.at[to_y], yq.at[y], ys_s.at[k], ys_r.at[y], dev(x, to_y, z, c)),
            remote(gzb.at[to_z], zq.at[z], zq_s.at[k], zq_r.at[z], dev(x, y, to_z, c)),
        )

    def sum_start(k, _):
        for copy in sum_copies(k):
            copy.start()
        return 0

    lax.fori_loop(1, 8, sum_start, 0)
    ya[...] = gyf[y]
    za[...] = gzf[z]

    def sum_add(k, _):
        from_y, from_z = lax.rem(y + k, NY), lax.rem(z + k, NZ)
        remote(yq.at[from_y], yq.at[from_y], ys_s.at[k], ys_r.at[from_y], sib).wait_recv()
        ya[...] += yq[from_y].astype(F32)
        remote(zq.at[from_z], zq.at[from_z], zq_s.at[k], zq_r.at[from_z], sib).wait_recv()
        za[...] += zq[from_z].astype(F32)
        return 0

    lax.fori_loop(1, 8, sum_add, 0)

    def window(ref, i):
        start = lax.div(i, 2) * 2 * PIECE + lax.rem(i, 2) * 32
        return ref.at[pl.ds(pl.multiple_of(start, 8), WIN)]

    def last_copies(k):
        to_z, to_y = lax.rem(z + k, NZ), lax.rem(y + k, NY)
        return (
            remote(window(ya, to_z), y2.at[z], zr_s.at[k], zr_r.at[z], dev(x, y, to_z, c)),
            remote(window(za, to_y), z2.at[y], yr_s.at[k], yr_r.at[y], dev(x, to_y, z, c)),
        )

    def last_start(k, _):
        for copy in last_copies(k):
            copy.start()
        return 0

    def last_wait(k, _):
        from_z, from_y = lax.rem(z + k, NZ), lax.rem(y + k, NY)
        remote(y2.at[from_z], y2.at[from_z], zr_s.at[k], zr_r.at[from_z], sib).wait_recv()
        remote(z2.at[from_y], z2.at[from_y], yr_s.at[k], yr_r.at[from_y], sib).wait_recv()
        return 0

    lax.fori_loop(1, 8, last_start, 0)
    y2[z] = window(ya, z)[...]
    z2[y] = window(za, y)[...]
    lax.fori_loop(1, 8, last_wait, 0)

    def piece_of(ref, odd):
        total = jnp.sum(ref[...], axis=0)
        return jnp.where(odd == 0, total[:PIECE], total[WIN - PIECE :])

    ow[:PIECE] = jnp.concatenate([piece_of(y2, zl), piece_of(z2, lax.rem(y, 2))], axis=1)
    ow[PIECE:] = jnp.zeros((WIN - PIECE, SLAB), F32)

    @pl.when(away)
    def _():
        copy = remote(ow, ox, o_s, o_r, partner)
        copy.start()
        copy.wait()

    @pl.when(jnp.logical_not(away))
    def _():
        ox[...] = ow[...]

    out_ref[...] = ox[:PIECE]

    for d in (0, 1):
        for a in (0, 1):
            for h in (0, 1):
                send_own(d, h, a).wait_send()
            pass_on(d, a).wait_send()
    for a in (0, 1):
        for h in (0, 1):
            own_to_sib(h, a).wait_send()
            for n, block in ((1, xl), (2, xr), (3, xo)):
                to_sib(n, block, h, a).wait_send()
    for step in range(4):
        for d in (0, 1):
            for h in (0, 1):
                if step < 3 or h == d:
                    for a in (0, 1):
                        ring_copy(a, d, step, h, False).wait_send()

    def wait_sent(k, _):
        remote(labs.at[me], labs.at[me], lab_s.at[k], lab_r.at[me], sib).wait_send()
        for copy in z_copies(k, False):
            copy.wait_send()
        late_copy(k, me).wait_send()
        for copy in sum_copies(k) + last_copies(k):
            copy.wait_send()
        return 0

    lax.fori_loop(1, 8, wait_sent, 0)


def per_device(teacher_hidden, student_hidden, teacher_head, student_head, targets, row_mask):
    dt, ds = teacher_hidden.shape[1], student_hidden.shape[1]
    bf16 = jnp.bfloat16
    dma = pltpu.SemaphoreType.DMA
    anywhere, vmem = pl.BlockSpec(memory_space=pl.ANY), pl.BlockSpec(memory_space=pltpu.VMEM)
    loss, out = pl.pallas_call(
        kernel,
        out_shape=(jax.ShapeDtypeStruct((1, ROWS), F32), jax.ShapeDtypeStruct((PIECE, SLAB), F32)),
        in_specs=[anywhere, anywhere, anywhere, vmem, vmem, vmem],
        out_specs=(vmem, vmem),
        scratch_shapes=[
            pltpu.VMEM((8, ROWS, dt), bf16),
            pltpu.VMEM((8, ROWS, ds), bf16),
            pltpu.VMEM((PAD, SLAB), bf16),
            pltpu.VMEM((SLAB, dt), bf16),
            pltpu.VMEM((NZ, NY, PAD, SLAB), bf16),
            pltpu.VMEM((ds, SLAB), bf16),
            pltpu.VMEM((SLAB, ds), bf16),
            pltpu.VMEM((ds, 8 * ROWS), bf16),
            pltpu.VMEM((NX, SLAB, 2 * ROWS), F32),
            pltpu.VMEM((NX, SLAB, 2 * ROWS), F32),
            pltpu.VMEM((SLAB, 8 * ROWS), bf16),
            pltpu.VMEM((NY, CHUNK, 128), F32),
            pltpu.VMEM((NY, CHUNK, 128), bf16),
            pltpu.VMEM((NZ, CHUNK, 128), F32),
            pltpu.VMEM((NZ, CHUNK, 128), bf16),
            pltpu.VMEM((NY, CHUNK, 128), bf16),
            pltpu.VMEM((NZ, CHUNK, 128), bf16),
            pltpu.VMEM((CHUNK, 128), F32),
            pltpu.VMEM((CHUNK, 128), F32),
            pltpu.VMEM((NZ, WIN, 128), F32),
            pltpu.VMEM((NY, WIN, 128), F32),
            pltpu.VMEM((WIN, SLAB), F32),
            pltpu.VMEM((WIN, SLAB), F32),
            pltpu.VMEM((8, 8, ROWS), jnp.int32),
            pltpu.VMEM((8, NX, 8, 2 * ROWS), F32),
            pltpu.VMEM((8, 8, 2 * ROWS), F32),
            pltpu.VMEM((8, 1, ROWS), F32),
            dma((4,)),
            dma((8,)), dma((8,)),
            dma((2,)), dma((2,)),
            dma((8,)), dma((8,)), dma((8,)), dma((8,)),
            dma((2, 2, 4, 2)), dma((2, 2, 4, 2)),
            dma((2, 2, 2)), dma((2, 2, 2)),
            dma((2, 2)), dma((2, 2)),
            dma((4, 2, 2)), dma((4, 2, 2)),
            dma((8,)), dma((8,)), dma((8,)), dma((8,)),
            dma((8,)), dma((8,)), dma((8,)), dma((8,)),
            dma((8,)), dma((8,)), dma((8,)), dma((8,)),
            dma, dma,
        ],
        compiler_params=pltpu.CompilerParams(
            collective_id=0, has_side_effects=True, vmem_limit_bytes=56 * 1024 * 1024
        ),
        cost_estimate=pl.CostEstimate(flops=4_900_000_000, bytes_accessed=6_000_000, transcendentals=1_000_000),
    )(teacher_hidden, student_hidden, teacher_head, student_head, targets.reshape(1, ROWS), row_mask.reshape(1, ROWS))
    return loss.reshape(ROWS), out


def solution(mesh):
    in_specs = (
        P(("tok", "voc"), None),
        P(("tok", "voc"), None),
        P("voc", None),
        P("tok", "voc"),
        P(("tok", "voc")),
        P(("tok", "voc")),
    )
    out_specs = (P(("tok", "voc")), P("tok", "voc"))
    return jax.shard_map(
        per_device, mesh=mesh, in_specs=in_specs, out_specs=out_specs, check_vma=False
    )
```

```python
import jax
import jax.numpy as jnp
from jax import lax
from jax.experimental import pallas as pl
from jax.experimental.pallas import tpu as pltpu
from jax.sharding import PartitionSpec as P

NX, NY, NZ = 4, 8, 8
ROWS = 128
HALF = ROWS // 2
SLAB = 256
PIECE = 36
PAD = 48
WIN = 40
CHUNK = 8 * PIECE
FAR_FIRST = (4, 3, 5, 2, 6, 1, 7)
MESH = pl.DeviceIdType.MESH
F32 = jnp.float32
NT = (((1,), (1,)), ((), ()))


def remote(src, dst, send, recv, device):
    return pltpu.make_async_remote_copy(
        src_ref=src, dst_ref=dst, send_sem=send, recv_sem=recv, device_id=device, device_id_type=MESH
    )


def kernel(
    th, sh, tw, sw, target_in, mask_in, out_ref,
    rt, rs, piece_ref, tslab, spad, swt, swr, rst, et, es, lg, gyf, gyb, gzf, gzb, yq, zq, ya, za, y2, z2, ow, ox, labs, stats, late, losses,
    loc_sem, lab_s, lab_r, tr_s, tr_r, zt_s, zt_r, zs_s, zs_r, h_s, h_r,
    x_s, x_r, f_s, f_r, b_s, b_r, st_s, st_r, sl_s, sl_r, ys_s, ys_r, zq_s, zq_r, yr_s, yr_r, zr_s, zr_r, o_s, o_r,
):
    tok, voc = lax.axis_index("tok"), lax.axis_index("voc")
    x, y, zl = lax.div(tok, 16), lax.rem(lax.div(tok, 2), NY), lax.rem(tok, 2)
    zh, c = lax.div(voc, 2), lax.rem(voc, 2)
    z = zh * 2 + zl
    me = x * 2 + c

    def dev(dx, dy, dz, dc):
        return ((dx * NY + dy) * 2 + lax.rem(dz, 2), lax.div(dz, 2) * 2 + dc)

    def group_dev(i):
        return dev(lax.div(i, 2), y, z, lax.rem(i, 2))

    xr, xl, xo = lax.rem(x + 1, NX), lax.rem(x + 3, NX), lax.rem(x + 2, NX)
    right, left, sib = dev(xr, y, z, c), dev(xl, y, z, c), dev(x, y, z, 1 - c)
    up, down = dev(x, lax.rem(y + 1, NY), z, c), dev(x, lax.rem(y + NY - 1, NY), z, c)
    z_up, z_down = dev(x, y, lax.rem(z + 1, NZ), c), dev(x, y, lax.rem(z + NZ - 1, NZ), c)
    partner = dev(zh, y, x * 2 + zl, c)
    away = x != zh

    barrier = pltpu.get_barrier_semaphore()

    def greet(k, _):
        pl.semaphore_signal(barrier, inc=1, device_id=group_dev(lax.rem(me + k, 8)), device_id_type=MESH)
        pl.semaphore_signal(barrier, inc=1, device_id=dev(x, y, lax.rem(z + k, NZ), c), device_id_type=MESH)
        pl.semaphore_signal(barrier, inc=1, device_id=dev(x, lax.rem(y + k, NY), z, c), device_id_type=MESH)
        return 0

    lax.fori_loop(1, 8, greet, 0)

    @pl.when(away)
    def _():
        pl.semaphore_signal(barrier, inc=1, device_id=partner, device_id_type=MESH)

    own_copies = [pltpu.make_async_copy(ref, dst.at[me], loc_sem.at[a]) for a, (ref, dst) in enumerate(((sh, rs), (th, rt)))]
    for copy in own_copies:
        copy.start()
    piece_ref[...] = jnp.concatenate([sw[...], jnp.zeros((PAD - PIECE, SLAB), sw.dtype)], axis=0)
    stats[me] = jnp.zeros(stats.shape[1:], F32)
    labs[me] = jnp.concatenate([target_in[...], mask_in[...], jnp.zeros((6, ROWS), jnp.int32)], axis=0)

    @pl.when(away)
    def _():
        pl.semaphore_wait(barrier, 22)

    @pl.when(jnp.logical_not(away))
    def _():
        pl.semaphore_wait(barrier, 21)

    t_row = pl.multiple_of(y * 32 + zl * 16, 16)

    def t_piece(ref, col):
        return ref.at[pl.ds(t_row, 16), pl.ds(pl.multiple_of(col * 1152, 128), 1152)]

    def turn(dst_col):
        src_t, dst_t = t_piece(tw, x), t_piece(tslab, dst_col)
        dst_s = spad.at[dst_col * 2 + zl, y]
        return src_t, dst_t, dst_s

    def turn_copies():
        src_t, dst_t, dst_s = turn(x)
        return (
            remote(src_t, dst_t, tr_s.at[0], tr_r.at[0], partner),
            remote(piece_ref, dst_s, tr_s.at[1], tr_r.at[1], partner),
        )

    def turn_local():
        src_t, dst_t, dst_s = turn(x)
        return (
            pltpu.make_async_copy(src_t, dst_t, loc_sem.at[2]),
            pltpu.make_async_copy(piece_ref, dst_s, loc_sem.at[3]),
        )

    def half(ref, block, h):
        return ref.at[block, pl.ds(h * HALF, HALF)]

    pairs = ((sh, rs), (th, rt))

    def send_own(d, h, a):
        src, dst = pairs[a]
        return remote(
            src.at[pl.ds(h * HALF, HALF)], half(dst, me, h), x_s.at[d, h, a], x_r.at[d, h, a], (right, left)[d]
        )

    def came_own(d, h, a):
        block = (xl, xr)[d] * 2 + c
        piece = half(pairs[a][1], block, h)
        return remote(piece, piece, x_s.at[d, h, a], x_r.at[d, h, a], (right, left)[d])

    def pass_on(d, a):
        block = (xl, xr)[d] * 2 + c
        piece = half(pairs[a][1], block, d)
        return remote(piece, piece, f_s.at[d, a], f_r.at[d, a], (right, left)[d])

    def came_on(d, a):
        piece = half(pairs[a][1], xo * 2 + c, d)
        return remote(piece, piece, f_s.at[d, a], f_r.at[d, a], (right, left)[d])

    def to_sib(n, block, h, a):
        piece = half(pairs[a][1], block * 2 + c, h)
        return remote(piece, piece, b_s.at[n, h, a], b_r.at[n, h, a], sib)

    def from_sib(n, block, h, a):
        piece = half(pairs[a][1], block * 2 + 1 - c, h)
        return remote(piece, piece, b_s.at[n, h, a], b_r.at[n, h, a], sib)

    def own_to_sib(h, a):
        src, dst = pairs[a]
        return remote(src.at[pl.ds(h * HALF, HALF)], half(dst, me, h), b_s.at[0, h, a], b_r.at[0, h, a], sib)

    for first in (0, 1):
        for a in (1, 0):
            send_own(0, first, a).start()
            send_own(1, 1 - first, a).start()
    @pl.when(away)
    def _():
        for copy in turn_copies():
            copy.start()

    @pl.when(jnp.logical_not(away))
    def _():
        for copy in turn_local():
            copy.start()

    for h in (0, 1):
        for a in (0, 1):
            own_to_sib(h, a).start()

    def send_labels(k, _):
        to = lax.rem(me + k, 8)
        remote(labs.at[me], labs.at[me], lab_s.at[k], lab_r.at[me], group_dev(to)).start()
        return 0

    lax.fori_loop(1, 8, send_labels, 0)

    @pl.when(away)
    def _():
        for copy in turn_copies():
            copy.wait_send()
        src_t, dst_t, dst_s = turn(zh)
        remote(dst_t, dst_t, tr_s.at[0], tr_r.at[0], partner).wait_recv()
        remote(dst_s, dst_s, tr_s.at[1], tr_r.at[1], partner).wait_recv()

    @pl.when(jnp.logical_not(away))
    def _():
        for copy in turn_local():
            copy.wait()

    def z_piece(dz):
        rows = pl.ds(pl.multiple_of(y * 32 + lax.rem(dz, 2) * 16, 16), 16)
        return tslab.at[rows, pl.ds(pl.multiple_of(lax.div(dz, 2) * 1152, 128), 1152)]

    def z_copies(k, back):
        dz, dy = lax.rem(z + k, NZ), lax.rem(y + k, NY)
        sz, sy = (dz, dy) if back else (z, y)
        t, s = z_piece(sz), spad.at[z, sy]
        return (
            remote(t, t, zt_s.at[k], zt_r.at[sz], dev(x, y, dz, c)),
            remote(s, s, zs_s.at[k], zs_r.at[sy], dev(x, dy, z, c)),
        )

    def z_start(k, _):
        for copy in z_copies(k, False):
            copy.start()
        return 0

    def z_wait(k, _):
        for copy in z_copies(k, True):
            copy.wait_recv()
        return 0

    lax.fori_loop(1, NZ, z_start, 0)
    lax.fori_loop(1, NZ, z_wait, 0)

    def ring_copy(a, d, step, h, back):
        gap = step + 1 if back else step
        move = (8 - gap, gap)[d]
        if a == 0:
            chunk = lax.rem(y + move, NY)
            piece = tslab.at[pl.ds(pl.multiple_of(chunk * 32 + 16 * h, 16), 16)]
        else:
            piece = spad.at[lax.rem(z + move, NZ), pl.ds(4 * h, 4)]
        to = ((up, down), (z_up, z_down))[a][d]
        return remote(piece, piece, h_s.at[a, d, step, h], h_r.at[a, d, step, h], to)

    def ring_step(step):
        for h in (0, 1):
            for d in (0, 1):
                for a in (0, 1):
                    if 0 < step < 4 or (step == 4 and h == d):
                        ring_copy(a, d, step - 1, h, True).wait_recv()
                    if step < 3 or (step == 3 and h == d):
                        ring_copy(a, d, step, h, False).start()

    ring_step(0)
    ring_step(1)
    for a in (1, 0):
        for d in (0, 1):
            came_own(d, d, a).wait_recv()
            pass_on(d, a).start()
            to_sib(1 + d, (xl, xr)[d], d, a).start()
    ring_step(2)
    ring_step(3)
    for a in (0, 1):
        for d in (0, 1):
            came_own(d, 1 - d, a).wait_recv()
            to_sib(1 + d, (xl, xr)[d], 1 - d, a).start()
    ring_step(4)

    r_out = lax.broadcasted_iota(jnp.int32, (4 * PAD, 4 * PIECE), 1)
    r_in = lax.broadcasted_iota(jnp.int32, (4 * PAD, 4 * PIECE), 0)
    quarter = lax.div(r_out, PIECE)
    pick = (r_in == quarter * PAD + (r_out - quarter * PIECE)).astype(jnp.bfloat16)

    for col in range(NX):
        parts = []
        for pair in range(NY // 2):
            four = [spad[2 * col + low, row] for row in (2 * pair, 2 * pair + 1) for low in (0, 1)]
            padded = jnp.concatenate(four, axis=0)
            parts.append(lax.dot_general(pick, padded, (((0,), (0,)), ((), ())), preferred_element_type=F32))
        swt[576 * col : 576 * (col + 1), :] = jnp.concatenate(parts, axis=0).astype(jnp.bfloat16)
    swr[...] = swt[...].T

    def wait_labels(k, _):
        other = lax.rem(me + k, 8)
        remote(labs.at[other], labs.at[other], lab_s.at[k], lab_r.at[other], sib).wait_recv()
        return 0

    lax.fori_loop(1, 8, wait_labels, 0)
    for copy in own_copies:
        copy.wait()
    for h in (0, 1):
        for a in (0, 1):
            from_sib(0, x, h, a).wait_recv()

    entry = lax.broadcasted_iota(jnp.int32, (SLAB, 2 * ROWS), 0) + me * SLAB

    def label_row(block, i):
        return jnp.concatenate([labs[2 * block, i : i + 1, :], labs[2 * block + 1, i : i + 1, :]], axis=1)

    def logits(block, sums):
        rows_t = rt[pl.ds(2 * block, 2)].reshape(2 * ROWS, rt.shape[2])
        lt = lax.dot_general(tslab[...], rows_t, NT, preferred_element_type=F32)
        rows_s = rs[pl.ds(2 * block, 2)].reshape(2 * ROWS, rs.shape[2])
        ls = lax.dot_general(swr[...], rows_s, NT, preferred_element_type=F32)
        rst[:, pl.ds(pl.multiple_of(block * 2 * ROWS, 2 * ROWS), 2 * ROWS)] = rows_s.T
        top_t = jnp.max(lt, axis=0, keepdims=True)
        top_s = jnp.max(ls, axis=0, keepdims=True)
        exp_t, exp_s = jnp.exp(lt - top_t), jnp.exp(ls - top_s)
        hit = entry == label_row(block, 0)
        et[block] = exp_t
        es[block] = exp_s
        sums[...] = jnp.concatenate(
            [
                top_t,
                top_s,
                jnp.sum(exp_t, axis=0, keepdims=True),
                jnp.sum(exp_t * (lt - ls), axis=0, keepdims=True),
                jnp.sum(exp_s, axis=0, keepdims=True),
                jnp.sum(jnp.where(hit, ls, 0.0), axis=0, keepdims=True),
                jnp.zeros((2, 2 * ROWS), F32),
            ],
            axis=0,
        )

    logits(x, stats.at[me, x])
    for d in (0, 1):
        for h in (0, 1):
            for a in (0, 1):
                from_sib(1 + d, (xl, xr)[d], h, a).wait_recv()
        logits((xl, xr)[d], stats.at[me, (xl, xr)[d]])
    def early_copy(k, slot):
        return remote(stats.at[slot], stats.at[slot], st_s.at[k], st_r.at[slot], group_dev(lax.rem(me + k, 8)))

    def late_copy(k, slot):
        return remote(late.at[slot], late.at[slot], sl_s.at[k], sl_r.at[slot], group_dev(lax.rem(me + k, 8)))

    def send_early(k, _):
        early_copy(k, me).start()
        return 0

    def send_stats(k, _):
        late_copy(k, me).start()
        return 0

    def wait_stats(k, _):
        other = lax.rem(me + k, 8)
        early_copy(k, me).wait_send()
        early_copy(k, other).wait_recv()
        late_copy(k, other).wait_recv()
        return 0

    lax.fori_loop(1, 8, send_early, 0)
    for a in (1, 0):
        for d in (0, 1):
            came_on(d, a).wait_recv()
            to_sib(3, xo, d, a).start()
    for d in (0, 1):
        for a in (0, 1):
            from_sib(3, xo, d, a).wait_recv()
    logits(xo, late.at[me])

    lax.fori_loop(1, 8, send_stats, 0)
    lax.fori_loop(1, 8, wait_stats, 0)
    for sender in range(8):
        stats[sender, (sender // 2 + 2) % NX] = late[sender]

    for block in range(NX):
        tops_t, tops_s = stats[:, block, 0, :], stats[:, block, 1, :]
        top_t = jnp.max(tops_t, axis=0, keepdims=True)
        top_s = jnp.max(tops_s, axis=0, keepdims=True)
        scale_t, scale_s = jnp.exp(tops_t - top_t), jnp.exp(tops_s - top_s)
        sum_t = jnp.sum(stats[:, block, 2, :] * scale_t, axis=0, keepdims=True)
        cross = jnp.sum(stats[:, block, 3, :] * scale_t, axis=0, keepdims=True)
        sum_s = jnp.sum(stats[:, block, 4, :] * scale_s, axis=0, keepdims=True)
        target = jnp.sum(stats[:, block, 5, :], axis=0, keepdims=True)
        lse_t, lse_s = top_t + jnp.log(sum_t), top_s + jnp.log(sum_s)
        weight = label_row(block, 1).astype(F32)
        loss = weight * (cross / sum_t - lse_t + lse_s + 0.5 * (lse_s - target))
        losses[2 * block] = loss[:, :ROWS]
        losses[2 * block + 1] = loss[:, ROWS:]
        prob_t = et[block] * (jnp.exp(stats[me, block, 0:1, :] - top_t) / sum_t)
        prob_s = es[block] * (jnp.exp(stats[me, block, 1:2, :] - top_s) / sum_s)
        onehot = (entry == label_row(block, 0)).astype(F32)
        grad = weight * ((prob_s - prob_t) + 0.5 * (prob_s - onehot))
        lg[:, 2 * ROWS * block : 2 * ROWS * (block + 1)] = grad.astype(jnp.bfloat16)
    own_loss = losses[me]

    half_cols = rst.shape[0] // 2
    for j in range(2):
        tile = lax.dot_general(
            rst[half_cols * j : half_cols * (j + 1), :], lg[...], NT, preferred_element_type=F32
        ).reshape(2, NY, 2 * PIECE, SLAB)
        for i in range(NY):
            part = jnp.concatenate([tile[0, i, :, :128], tile[1, i, :, :128]], axis=0)
            gyf[i, 4 * PIECE * j : 4 * PIECE * (j + 1)] = part
            gyb[i, 4 * PIECE * j : 4 * PIECE * (j + 1)] = part.astype(jnp.bfloat16)
        for a in (0, 1):
            for low in (0, 1):
                part = jnp.concatenate([tile[a, i, low * PIECE : (low + 1) * PIECE, 128:] for i in range(NY)], axis=0)
                gzf[4 * j + 2 * a + low] = part
                gzb[4 * j + 2 * a + low] = part.astype(jnp.bfloat16)

    def sum_copies(k):
        to_y, to_z = lax.rem(y + k, NY), lax.rem(z + k, NZ)
        return (
            remote(gyb.at[to_y], yq.at[y], ys_s.at[k], ys_r.at[y], dev(x, to_y, z, c)),
            remote(gzb.at[to_z], zq.at[z], zq_s.at[k], zq_r.at[z], dev(x, y, to_z, c)),
        )

    def sum_start(k, _):
        for copy in sum_copies(k):
            copy.start()
        return 0

    for k in FAR_FIRST:
        sum_start(k, 0)
    ya[...] = gyf[y]
    za[...] = gzf[z]

    def sum_add(k, _):
        from_y, from_z = lax.rem(y + k, NY), lax.rem(z + k, NZ)
        remote(yq.at[from_y], yq.at[from_y], ys_s.at[k], ys_r.at[from_y], sib).wait_recv()
        ya[...] += yq[from_y].astype(F32)
        remote(zq.at[from_z], zq.at[from_z], zq_s.at[k], zq_r.at[from_z], sib).wait_recv()
        za[...] += zq[from_z].astype(F32)
        return 0

    lax.fori_loop(1, 8, sum_add, 0)

    def window(ref, i):
        start = lax.div(i, 2) * 2 * PIECE + lax.rem(i, 2) * 32
        return ref.at[pl.ds(pl.multiple_of(start, 8), WIN)]

    def last_copies(k):
        to_z, to_y = lax.rem(z + k, NZ), lax.rem(y + k, NY)
        return (
            remote(window(ya, to_z), y2.at[z], zr_s.at[k], zr_r.at[z], dev(x, y, to_z, c)),
            remote(window(za, to_y), z2.at[y], yr_s.at[k], yr_r.at[y], dev(x, to_y, z, c)),
        )

    def last_start(k, _):
        for copy in last_copies(k):
            copy.start()
        return 0

    def last_wait(k, _):
        from_z, from_y = lax.rem(z + k, NZ), lax.rem(y + k, NY)
        remote(y2.at[from_z], y2.at[from_z], zr_s.at[k], zr_r.at[from_z], sib).wait_recv()
        remote(z2.at[from_y], z2.at[from_y], yr_s.at[k], yr_r.at[from_y], sib).wait_recv()
        return 0

    for k in FAR_FIRST:
        last_start(k, 0)
    y2[z] = window(ya, z)[...]
    z2[y] = window(za, y)[...]
    lax.fori_loop(1, 8, last_wait, 0)

    def piece_of(ref, odd):
        total = jnp.sum(ref[...], axis=0)
        return jnp.where(odd == 0, total[:PIECE], total[WIN - PIECE :])

    ow[:PIECE] = jnp.concatenate([piece_of(y2, zl), piece_of(z2, lax.rem(y, 2))], axis=1)
    ow[PIECE:] = jnp.zeros((WIN - PIECE, SLAB), F32)
    out_ref[PIECE:] = jnp.zeros((WIN - PIECE, SLAB), F32)

    @pl.when(away)
    def _():
        copy = remote(ow, ox, o_s, o_r, partner)
        copy.start()
        copy.wait()

    @pl.when(jnp.logical_not(away))
    def _():
        ox[...] = ow[...]

    out_ref[:PIECE] = ox[:PIECE]
    out_ref[PIECE : PIECE + 1] = jnp.concatenate([own_loss, own_loss], axis=1)

    for d in (0, 1):
        for a in (0, 1):
            for h in (0, 1):
                send_own(d, h, a).wait_send()
            pass_on(d, a).wait_send()
    for a in (0, 1):
        for h in (0, 1):
            own_to_sib(h, a).wait_send()
            for n, block in ((1, xl), (2, xr), (3, xo)):
                to_sib(n, block, h, a).wait_send()
    for step in range(4):
        for d in (0, 1):
            for h in (0, 1):
                if step < 3 or h == d:
                    for a in (0, 1):
                        ring_copy(a, d, step, h, False).wait_send()

    def wait_sent(k, _):
        remote(labs.at[me], labs.at[me], lab_s.at[k], lab_r.at[me], sib).wait_send()
        for copy in z_copies(k, False):
            copy.wait_send()
        late_copy(k, me).wait_send()
        for copy in sum_copies(k) + last_copies(k):
            copy.wait_send()
        return 0

    lax.fori_loop(1, 8, wait_sent, 0)


def per_device(teacher_hidden, student_hidden, teacher_head, student_head, targets, row_mask):
    dt, ds = teacher_hidden.shape[1], student_hidden.shape[1]
    bf16 = jnp.bfloat16
    dma = pltpu.SemaphoreType.DMA
    anywhere, vmem = pl.BlockSpec(memory_space=pl.ANY), pl.BlockSpec(memory_space=pltpu.VMEM)
    out = pl.pallas_call(
        kernel,
        out_shape=jax.ShapeDtypeStruct((WIN, SLAB), F32),
        in_specs=[anywhere, anywhere, anywhere, vmem, vmem, vmem],
        out_specs=vmem,
        scratch_shapes=[
            pltpu.VMEM((8, ROWS, dt), bf16),
            pltpu.VMEM((8, ROWS, ds), bf16),
            pltpu.VMEM((PAD, SLAB), bf16),
            pltpu.VMEM((SLAB, dt), bf16),
            pltpu.VMEM((NZ, NY, PAD, SLAB), bf16),
            pltpu.VMEM((ds, SLAB), bf16),
            pltpu.VMEM((SLAB, ds), bf16),
            pltpu.VMEM((ds, 8 * ROWS), bf16),
            pltpu.VMEM((NX, SLAB, 2 * ROWS), F32),
            pltpu.VMEM((NX, SLAB, 2 * ROWS), F32),
            pltpu.VMEM((SLAB, 8 * ROWS), bf16),
            pltpu.VMEM((NY, CHUNK, 128), F32),
            pltpu.VMEM((NY, CHUNK, 128), bf16),
            pltpu.VMEM((NZ, CHUNK, 128), F32),
            pltpu.VMEM((NZ, CHUNK, 128), bf16),
            pltpu.VMEM((NY, CHUNK, 128), bf16),
            pltpu.VMEM((NZ, CHUNK, 128), bf16),
            pltpu.VMEM((CHUNK, 128), F32),
            pltpu.VMEM((CHUNK, 128), F32),
            pltpu.VMEM((NZ, WIN, 128), F32),
            pltpu.VMEM((NY, WIN, 128), F32),
            pltpu.VMEM((WIN, SLAB), F32),
            pltpu.VMEM((WIN, SLAB), F32),
            pltpu.VMEM((8, 8, ROWS), jnp.int32),
            pltpu.VMEM((8, NX, 8, 2 * ROWS), F32),
            pltpu.VMEM((8, 8, 2 * ROWS), F32),
            pltpu.VMEM((8, 1, ROWS), F32),
            dma((4,)),
            dma((8,)), dma((8,)),
            dma((2,)), dma((2,)),
            dma((8,)), dma((8,)), dma((8,)), dma((8,)),
            dma((2, 2, 4, 2)), dma((2, 2, 4, 2)),
            dma((2, 2, 2)), dma((2, 2, 2)),
            dma((2, 2)), dma((2, 2)),
            dma((4, 2, 2)), dma((4, 2, 2)),
            dma((8,)), dma((8,)), dma((8,)), dma((8,)),
            dma((8,)), dma((8,)), dma((8,)), dma((8,)),
            dma((8,)), dma((8,)), dma((8,)), dma((8,)),
            dma, dma,
        ],
        compiler_params=pltpu.CompilerParams(
            collective_id=0, has_side_effects=True, vmem_limit_bytes=56 * 1024 * 1024
        ),
        cost_estimate=pl.CostEstimate(flops=4_900_000_000, bytes_accessed=6_000_000, transcendentals=1_000_000),
    )(teacher_hidden, student_hidden, teacher_head, student_head, targets.reshape(1, ROWS), row_mask.reshape(1, ROWS))
    return out[PIECE, :ROWS], out[:PIECE]


def solution(mesh):
    in_specs = (
        P(("tok", "voc"), None),
        P(("tok", "voc"), None),
        P("voc", None),
        P("tok", "voc"),
        P(("tok", "voc")),
        P(("tok", "voc")),
    )
    out_specs = (P(("tok", "voc")), P("tok", "voc"))
    return jax.shard_map(
        per_device, mesh=mesh, in_specs=in_specs, out_specs=out_specs, check_vma=False
    )
```
